1024 devices in a mesh: expert: 32 (over z_hi, x), dp: 32 (over y, z_lo, core).
Axes of the slice: x: 8, y: 8, z: 8 (z_hi: 4, z_lo: 2; z = z_hi * 2 + z_lo), core: 2. Of those that a mesh axis runs over, the one named last changes fastest.
Arguments:
- grad_output: bfloat16 [131072, 2048], P(('expert', 'dp')), may hold values from -1.5 to 1.5
- logits: float32 [131072, 8], P(('expert', 'dp')), may hold values from -6 to 6
- chosen: int32 [131072, 8], P(('expert', 'dp')), may hold values from 0 to 127, as said below
- slots: int32 [131072, 8], P(('expert', 'dp')), may hold values from 0 to 10, as said below
- other_scores: float32 [131072, 8], P(('expert', 'dp')), may hold values from -48 to 48
- hidden: bfloat16 [32, 32, 32, 10, 768], P('expert', 'dp'), may hold values from -6 to 6
- down_weight: bfloat16 [32, 768, 2048], P('expert', 'dp'), may hold values from -0.21875 to 0.21875
Outputs:
- grad_hidden: bfloat16 [32, 32, 32, 10, 768], P('expert', 'dp')
- grad_down: float32 [32, 768, 2048], P('expert', 'dp')
- grad_logits: float32 [131072, 8], P(('expert', 'dp'))
The draws below stay inside these ranges and needn't reach their ends.
Inputs may be any that keep to these rules, and one draw needn't show every extreme that they name: `chosen`: each row names 8 different experts. 10 marks a choice with no slot: its expert is 32 or above, or it comes after 10 earlier choices of the same expert among the rows of one device in row-major order. The live choices of one expert on one device hold slots 0, 1, 2, ... in that order. Some expert fills all 10 slots on some device.
All inputs are finite; a program needn't handle non-finite values.
Results may differ from the reference program's by a relative error of at most 0.023.
Values may be sent and summed in bfloat16 or wider, within the bound.
No kernel may reach another device: no remote copies, remote signals or barrier semaphores. Data moves between devices by JAX's collectives and lax.ppermute only.
A program may use at most 32 MiB of HBM per device.

```python
import jax
import jax.numpy as jnp
from jax import lax

D = 2048
FF = 768
TOPK = 8
TOK_DEV = 128
EXPERTS = 128
WINDOW = 32
CAP = 10
TOKENS = 131072
N_EXPERT = 32
N_DP = 32


def route_table(key):
    inner_key = jax.random.fold_in(key, 11)
    random_bits = jax.random.randint(inner_key, (TOKENS, EXPERTS), 0, 1 << 20)
    ranking = random_bits * EXPERTS + jnp.arange(EXPERTS, dtype=jnp.int32)[None, :]
    unused, picked = lax.top_k(ranking, TOPK)
    picked = picked.astype(jnp.int32)
    blocks = picked.reshape(TOKENS // TOK_DEV, TOK_DEV * TOPK)
    onehot = (blocks[:, :, None] == jnp.arange(WINDOW, dtype=jnp.int32)[None, None, :]).astype(jnp.int32)
    ranks = jnp.cumsum(onehot, axis=1) - 1
    position = jnp.sum(ranks * onehot, axis=2)
    inside = (blocks < WINDOW) & (position < CAP)
    placed = jnp.where(inside, position, CAP).astype(jnp.int32)
    return (picked, placed.reshape(TOKENS, TOPK))


def draw_chosen(key, part):
    picked, placed = route_table(key)
    return picked


def draw_slots(key, part):
    picked, placed = route_table(key)
    return placed


def block_levels(rng, extent, shards, smallest, top_value):
    def one(dim, shards_of):
        steps = jax.random.uniform(jax.random.fold_in(jax.random.fold_in(rng, 6), dim), (shards_of,), jnp.float32, smallest / len(shards), top_value / len(shards))
        return jnp.repeat(jnp.exp(steps), extent[dim] // shards_of).reshape((-1,) + (1,) * (len(extent) - dim - 1))

    gain = one(*shards[0])
    for cut in shards[1:]:
        gain = gain * one(*cut)
    return gain


def bell_draw(key, shape, width, reach, pieces=(), kind=jnp.bfloat16):
    factor_of = block_levels(key, shape, pieces, -0.22, 0.18) if pieces else 1.0
    values = jax.random.normal(key, shape, jnp.float32) * width * factor_of
    return jnp.minimum(jnp.maximum(values, -reach), reach).astype(kind)


def setup_inputs(seed: int = 0) -> dict:
    streams_of = jax.random.split(jax.random.key(seed), 8)
    return {
        "grad_output": bell_draw(streams_of[0], (TOKENS, D), 0.25, 1.5, ((0, 1024),)),
        "logits": bell_draw(streams_of[1], (TOKENS, TOPK), 1.0, 6.0, ((0, 1024),), jnp.float32),
        "chosen": draw_chosen(jax.random.fold_in(streams_of[7], 71), 0),
        "slots": draw_slots(jax.random.fold_in(streams_of[7], 71), 0),
        "other_scores": bell_draw(streams_of[4], (TOKENS, TOPK), 8.0, 48.0, ((0, 1024),), jnp.float32),
        "hidden": bell_draw(streams_of[5], (WINDOW, N_DP, N_EXPERT, CAP, FF), 1.0, 6.0, ((0, 32), (1, 32))),
        "down_weight": bell_draw(streams_of[6], (WINDOW, FF, D), FF ** -0.5, 0.21875, ((0, 32), (1, 32))),
    }


def reference(grad_output, logits, chosen, slots, other_scores, hidden, down_weight):
    raised = jnp.exp(logits)
    gating = raised / jnp.sum(raised, axis=1, keepdims=True)
    gate_sent = gating.astype(jnp.bfloat16)
    row_index = jnp.arange(TOKENS, dtype=jnp.int32)
    block_index = row_index // TOK_DEV
    source_index = block_index // N_DP
    shard_index = block_index % N_DP
    live_slot = slots < CAP
    slot_count = N_DP * N_EXPERT * CAP
    total_slots = WINDOW * slot_count
    flat_place = ((chosen * N_DP + shard_index[:, None]) * N_EXPERT + source_index[:, None]) * CAP + slots
    flat_place = jnp.where(live_slot, flat_place, total_slots).astype(jnp.int32).reshape(-1)
    pair_index = jnp.arange(TOKENS * TOPK, dtype=jnp.int32)
    owners = jnp.zeros((total_slots + 1,), jnp.int32).at[flat_place].set(pair_index)
    filled = jnp.zeros((total_slots + 1,), jnp.float32).at[flat_place].set(1.0)
    owners = owners[:total_slots].reshape(WINDOW, slot_count)
    filled = filled[:total_slots].reshape(WINDOW, slot_count)
    gate_flat = gate_sent.reshape(-1)

    def expert_pass(inputs):
        owner_rows, fill_rows, expert_hidden, expert_weight = inputs
        slot_mask = fill_rows.astype(jnp.bfloat16)
        slot_rows = grad_output[owner_rows // TOPK] * slot_mask[:, None]
        slot_gate = (gate_flat[owner_rows] * slot_mask).astype(jnp.float32)
        local_hidden = expert_hidden.reshape(slot_count, FF)
        upward = lax.dot_general(slot_rows, expert_weight, (((1,), (1,)), ((), ())), preferred_element_type=jnp.float32)
        grad_rows = (slot_gate[:, None] * upward).astype(jnp.bfloat16)
        outputs = jnp.dot(local_hidden, expert_weight, preferred_element_type=jnp.float32)
        slot_scores = jnp.sum(slot_rows.astype(jnp.float32) * outputs, axis=1)
        scaled = (slot_gate[:, None] * slot_rows.astype(jnp.float32)).astype(jnp.bfloat16)

        def add_shard(totals, shard):
            shard_hidden, shard_scaled = shard
            partial_value = lax.dot_general(shard_hidden, shard_scaled, (((0,), (0,)), ((), ())), preferred_element_type=jnp.float32)
            rounded = lax.optimization_barrier(partial_value.astype(jnp.bfloat16))
            return totals + rounded.astype(jnp.float32), None

        grads, unused = lax.scan(add_shard, jnp.zeros((FF, D), jnp.float32),
                                 (local_hidden.reshape(N_DP, N_EXPERT * CAP, FF), scaled.reshape(N_DP, N_EXPERT * CAP, D)))
        return grad_rows, grads, slot_scores

    grad_rows, grad_down, slot_scores = lax.map(expert_pass, (owners, filled, hidden, down_weight))
    grad_hidden = grad_rows.reshape(WINDOW, N_DP, N_EXPERT, CAP, FF)
    score_flat = jnp.concatenate([slot_scores.reshape(-1), jnp.zeros((1,), jnp.float32)])
    token_scores = score_flat[flat_place].reshape(TOKENS, TOPK)
    outside = jnp.where(chosen >= WINDOW, other_scores, jnp.float32(0.0))
    scores_all = jnp.where(live_slot, token_scores, outside)
    mean_score = jnp.sum(gating * scores_all, axis=1, keepdims=True)
    grad_logits = gating * (scores_all - mean_score)
    return grad_hidden, grad_down, grad_logits
```

```python
import functools

import jax
import jax.numpy as jnp
from jax import lax
from jax.experimental import pallas as pl
from jax.experimental.pallas import tpu as pltpu
from jax.sharding import Mesh
from jax.sharding import PartitionSpec as P

EXPERT = ("zh", "x")
RING = ("y", "zl")
DP = ("y", "zl", "core")
ALL = EXPERT + DP
CHUNKS = 2
FOLD = 4
F32 = jnp.float32
BF16 = jnp.bfloat16
VMEM = pl.BlockSpec(memory_space=pltpu.VMEM)
SMEM = pl.BlockSpec(memory_space=pltpu.SMEM)
PARAMS = pltpu.CompilerParams(vmem_limit_bytes=48 * 1024 * 1024)


def cost(flops, size):
    return pl.CostEstimate(flops=flops, bytes_accessed=size, transcendentals=0)


def iota(shape, dim):
    return lax.broadcasted_iota(jnp.int32, shape, dim)


def onehot(mask):
    return jnp.where(mask, 1.0, 0.0).astype(BF16)


def dot(a, b, ca=1, cb=0):
    return lax.dot_general(a, b, (((ca,), (cb,)), ((), ())), preferred_element_type=F32)


def softmax_rows(logits):
    raised = jnp.exp(logits)
    return raised / jnp.sum(raised, axis=0, keepdims=True)


def pack_kernel(logits_ref, chosen_ref, slots_ref, rows_ref, *out_refs):
    gate = softmax_rows(logits_ref[...]).astype(BF16).astype(F32)
    chosen, slots = chosen_ref[...], slots_ref[...]
    topk, tokens = chosen.shape
    rows = out_refs[0].shape[0]
    main = jnp.where(slots < 8, chosen * 8 + slots, -1)
    extra = jnp.where((slots >= 8) & (slots < 10), chosen * 2 + slots - 8, -1)
    row = iota((rows, tokens), 0)
    place = jnp.zeros((rows, tokens), F32)
    fold = jnp.zeros((rows, tokens), F32)
    for k in range(topk):
        place = jnp.where(row == main[k : k + 1, :], gate[k : k + 1, :], place)
        fold = jnp.where(row // FOLD == extra[k : k + 1, :], gate[k : k + 1, :], fold)
    place = place.astype(BF16)
    folds = [jnp.where(row % FOLD == m, fold, 0.0).astype(BF16) for m in range(FOLD)]
    width = rows_ref.shape[1] // len(out_refs)
    part = width // FOLD
    for j, out in enumerate(out_refs):
        block = rows_ref[:, j * width : (j + 1) * width]
        out[:, :width] = dot(place, block).astype(BF16)
        total = sum(dot(folds[m], block[:, m * part : (m + 1) * part]) for m in range(FOLD))
        out[:, width:] = total.astype(BF16)


def permuted_units(core, units, shard):
    half = units // 2
    place = iota((1, units), 1)
    other = (place >= half).astype(jnp.int32)
    inner = place - other * half
    side = jnp.where(other == 1, 1 - core, core)
    block = inner // shard
    return block * (2 * shard) + side * shard + (inner - block * shard)


def hidden_kernel(shard, core_ref, hidden_ref, main_ref, extra_ref, main_t_ref, extra_t_ref):
    rows, units = main_ref.shape
    to_unit = permuted_units(core_ref[0], units, shard)
    column = onehot(iota((units, units), 0) == to_unit)
    source = rows // 8
    here = iota((rows, rows), 0)
    there = iota((rows, rows), 1)
    turn = onehot(there == (here % 8) * source + here // 8)
    turned = dot(turn, hidden_ref[:rows, :]).astype(BF16)
    last = hidden_ref[rows:, :]
    main_ref[...] = dot(turned, column).astype(BF16)
    extra_ref[...] = dot(last, column).astype(BF16)
    main_t_ref[...] = dot(column, turned, 0, 1).astype(BF16)
    extra_t_ref[...] = dot(column, last, 0, 1).astype(BF16)


def unfolded(block, m):
    rows = block.shape[0]
    few = rows // FOLD
    source = rows // 8
    here = iota((few, rows), 0)
    there = iota((few, rows), 1)
    pick = onehot(there == (here % source) * 8 + (here // source) * FOLD + m)
    return dot(pick, block).astype(BF16)


def partial_kernel(main_t_ref, extra_t_ref, rows_ref, fold_ref, own_ref, other_ref):
    m = pl.program_id(0)
    half = own_ref.shape[0]
    total = dot(main_t_ref[...], rows_ref[...])
    total = total + dot(extra_t_ref[...], unfolded(fold_ref[...], m))
    own_ref[...] = total[:half, :].astype(BF16)
    other_ref[...] = total[half:, :].astype(BF16)


def partial_sums(main_t, extra_t, payload):
    units = main_t.shape[0]
    rows = payload.shape[0]
    width = payload.shape[1] * FOLD // (FOLD + 1)
    part = width // FOLD
    few = rows // FOLD
    out = jax.ShapeDtypeStruct((units // 2, width), BF16)
    return pl.pallas_call(
        partial_kernel,
        grid=(FOLD,),
        in_specs=[
            pl.BlockSpec((units, rows), lambda m: (0, 0)),
            pl.BlockSpec((units, few), lambda m: (0, 0)),
            pl.BlockSpec((rows, part), lambda m: (0, m)),
            pl.BlockSpec((rows, part), lambda m: (0, FOLD)),
        ],
        out_specs=[pl.BlockSpec((units // 2, part), lambda m: (0, m))] * 2,
        out_shape=[out, out],
        compiler_params=PARAMS,
        cost_estimate=cost(2 * units * (rows + few) * width, 4 * units * width),
        name="partial_sums",
    )(main_t, extra_t, payload, payload)


def product_kernel(shard, core_ref, main_ref, extra_ref, own_ref, other_ref, *refs):
    chunks = (len(refs) - 4) // 2
    payloads, (grad_ref, score_ref, acc_main, acc_extra) = refs[: 2 * chunks], refs[2 * chunks :]
    g = pl.program_id(0)
    rows, units = main_ref.shape
    half = units // 2
    few = rows // FOLD

    @pl.when(g == 0)
    def _():
        acc_main[...] = jnp.zeros_like(acc_main)
        acc_extra[...] = jnp.zeros_like(acc_extra)

    for j in range(chunks):

        @pl.when(g // FOLD == j)
        def _():
            block = payloads[2 * j][...]
            more = unfolded(payloads[2 * j + 1][...], g % FOLD)
            for h, weight in enumerate((own_ref[...], other_ref[...])):
                span = slice(h * half, (h + 1) * half)
                acc_main[:, span] += dot(block, weight, 1, 1)
                acc_extra[:, span] += dot(more, weight, 1, 1)

    @pl.when(g == chunks * FOLD - 1)
    def _():
        main, extra = acc_main[...], acc_extra[...]
        main_score = jnp.sum(main * main_ref[...].astype(F32), axis=1, keepdims=True)
        extra_score = jnp.sum(extra * extra_ref[...].astype(F32), axis=1, keepdims=True)
        source = rows // 8
        lane = iota((rows, 128), 1)
        spread = jnp.where(lane == iota((rows, 128), 0) % 8, main_score, 0.0)
        scores = jnp.sum(spread.reshape(source, 8, 128), axis=1)
        lane = iota((source, 128), 1)
        for c in range(2):
            scores = jnp.where(lane == 8 + c, extra_score[c * source : (c + 1) * source, :], scores)
        score_ref[...] = scores
        to_unit = permuted_units(core_ref[0], units, shard)
        column = onehot(iota((units, units), 0) == to_unit)
        here = iota((rows, rows), 0)
        there = iota((rows, rows), 1)
        turn = onehot(there == (here % source) * 8 + here // source)
        turned = dot(turn, main.astype(BF16)).astype(BF16)
        grad_ref[:rows, :] = dot(turned, column, 1, 1).astype(BF16)
        grad_ref[rows:, :] = dot(extra.astype(BF16), column, 1, 1).astype(BF16)


def products(core, shard, main, extra, own, other, payloads):
    rows, units = main.shape
    few = rows // FOLD
    chunks = len(payloads)
    width = payloads[0].shape[1] * FOLD // (FOLD + 1)
    part = width // FOLD

    def block_of(j):
        return lambda g: (0, jnp.clip(g - FOLD * j, 0, FOLD - 1))

    fixed = lambda g: (0, 0)
    specs = [
        SMEM,
        pl.BlockSpec((rows, units), fixed),
        pl.BlockSpec((few, units), fixed),
        pl.BlockSpec((units // 2, part), lambda g: (0, g)),
        pl.BlockSpec((units // 2, part), lambda g: (0, g)),
    ]
    operands = []
    for j, payload in enumerate(payloads):
        specs.append(pl.BlockSpec((rows, part), block_of(j)))
        specs.append(pl.BlockSpec((rows, part), lambda g: (0, FOLD)))
        operands += [payload, payload]
    return pl.pallas_call(
        functools.partial(product_kernel, shard),
        grid=(chunks * FOLD,),
        in_specs=specs,
        out_specs=[
            pl.BlockSpec((rows + few, units), fixed),
            pl.BlockSpec((rows // 8, 128), fixed),
        ],
        out_shape=[
            jax.ShapeDtypeStruct((rows + few, units), BF16),
            jax.ShapeDtypeStruct((rows // 8, 128), F32),
        ],
        scratch_shapes=[pltpu.VMEM((rows, units), F32), pltpu.VMEM((few, units), F32)],
        compiler_params=PARAMS,
        cost_estimate=cost(2 * units * (rows + few) * width * chunks, 4 * units * width * chunks),
        name="products",
    )(core, main, extra, own, other, *operands)


def logits_kernel(logits_ref, chosen_ref, slots_ref, outside_ref, score_ref, out_ref):
    gating = softmax_rows(logits_ref[...])
    sent = gating.astype(BF16).astype(F32)
    chosen, slots = chosen_ref[...], slots_ref[...]
    topk, tokens = chosen.shape
    experts = score_ref.shape[0]
    returned = score_ref[...]
    found = []
    for k in range(topk):
        hit = jnp.where(iota((experts, tokens), 0) == chosen[k : k + 1, :], 1.0, 0.0)
        by_slot = lax.dot_general(
            returned,
            hit,
            (((0,), (0,)), ((), ())),
            precision=lax.Precision.HIGHEST,
            preferred_element_type=F32,
        )[:16, :]
        at_slot = iota((16, tokens), 0) == slots[k : k + 1, :]
        found.append(jnp.sum(jnp.where(at_slot, by_slot, 0.0), axis=0, keepdims=True))
    inside = jnp.concatenate(found, axis=0) / sent
    outside = jnp.where(chosen >= experts, outside_ref[...], 0.0)
    scores = jnp.where(slots < 10, inside, outside)
    mean = jnp.sum(gating * scores, axis=0, keepdims=True)
    out_ref[...] = gating * (scores - mean)


def body(grad_output, logits, chosen, slots, other_scores, hidden, down_weight):
    tokens, topk = logits.shape
    window, capacity, units = hidden.shape[2], hidden.shape[3], hidden.shape[4]
    model = grad_output.shape[1]
    shard = down_weight.shape[1]
    width = model // CHUNKS
    core = lax.axis_index("core").astype(jnp.int32).reshape(1)
    logits_t, chosen_t, slots_t = logits.T, chosen.T, slots.T

    weights = down_weight.reshape(shard, model)
    own_weights = lax.all_gather(weights, RING).reshape(-1, model)
    other_weights = lax.ppermute(own_weights, "core", [(0, 1), (1, 0)])

    packed = pl.pallas_call(
        pack_kernel,
        in_specs=[VMEM] * 4,
        out_specs=[VMEM] * CHUNKS,
        out_shape=[jax.ShapeDtypeStruct((window * 8, width + width // FOLD), BF16)] * CHUNKS,
        compiler_params=PARAMS,
        cost_estimate=cost(2 * 320 * tokens * model * 2, 4 * 320 * model),
        name="pack",
    )(logits_t, chosen_t, slots_t, grad_output)
    payloads = []
    for part in packed:
        part = part.reshape(window, 8, part.shape[1])
        part = lax.all_to_all(part, EXPERT, split_axis=0, concat_axis=0, tiled=True)
        payloads.append(part.reshape(window * 8, part.shape[2]))

    by_slot = hidden.transpose(0, 1, 3, 2, 4).reshape(capacity * window, units)
    main, extra, main_t, extra_t = pl.pallas_call(
        functools.partial(hidden_kernel, shard),
        in_specs=[SMEM, VMEM],
        out_specs=[VMEM] * 4,
        out_shape=[
            jax.ShapeDtypeStruct((window * 8, units), BF16),
            jax.ShapeDtypeStruct((window * 2, units), BF16),
            jax.ShapeDtypeStruct((units, window * 8), BF16),
            jax.ShapeDtypeStruct((units, window * 2), BF16),
        ],
        compiler_params=PARAMS,
        cost_estimate=cost(4 * 320 * units * units, 8 * 320 * units),
        name="hidden_order",
    )(core, by_slot)

    sums = []
    for payload in payloads:
        own, other = partial_sums(main_t, extra_t, payload)
        arrived = lax.ppermute(other, "core", [(0, 1), (1, 0)])
        both = (own.astype(F32) + arrived.astype(F32)).astype(BF16)
        pieces = both.reshape(-1, shard, width)
        pieces = lax.all_to_all(pieces, RING, split_axis=0, concat_axis=0, tiled=True)
        sums.append(jnp.sum(pieces.astype(F32), axis=0))
    grad_down = jnp.concatenate(sums, axis=1).reshape(1, shard, model)

    grad, score = products(core, shard, main, extra, own_weights, other_weights, payloads)
    grad_hidden = grad.reshape(1, 1, capacity, window, units).transpose(0, 1, 3, 2, 4)
    returned = lax.all_to_all(
        score.reshape(window, 1, 128), EXPERT, split_axis=0, concat_axis=0, tiled=True
    ).reshape(window, 128)
    grad_logits = pl.pallas_call(
        logits_kernel,
        in_specs=[VMEM] * 5,
        out_specs=VMEM,
        out_shape=jax.ShapeDtypeStruct((topk, tokens), F32),
        compiler_params=PARAMS,
        name="logits",
    )(logits_t, chosen_t, slots_t, other_scores.T, returned)
    return grad_hidden, grad_down, grad_logits.T


def solution(mesh):
    torus = Mesh(mesh.devices.reshape(4, 8, 8, 2, 2), ALL)
    in_specs = (
        P(ALL, None),
        P(ALL, None),
        P(ALL, None),
        P(ALL, None),
        P(ALL, None),
        P(EXPERT, DP, None, None, None),
        P(EXPERT, DP, None),
    )
    out_specs = (P(EXPERT, DP, None, None, None), P(EXPERT, DP, None), P(ALL, None))
    return jax.shard_map(body, mesh=torus, in_specs=in_specs, out_specs=out_specs, check_vma=False)
```

```python
import functools

import jax
import jax.numpy as jnp
from jax import lax
from jax.experimental import pallas as pl
from jax.experimental.pallas import tpu as pltpu
from jax.sharding import Mesh
from jax.sharding import PartitionSpec as P

EXPERT = ("zh", "x")
RING = ("y", "zl")
DP = ("y", "zl", "core")
ALL = EXPERT + DP
FOLD = 4
F32 = jnp.float32
BF16 = jnp.bfloat16
VMEM = pl.BlockSpec(memory_space=pltpu.VMEM)
HBM = pl.BlockSpec(memory_space=pltpu.HBM)
SMEM = pl.BlockSpec(memory_space=pltpu.SMEM)
PARAMS = pltpu.CompilerParams(vmem_limit_bytes=48 * 1024 * 1024)


def cost(flops, size):
    return pl.CostEstimate(flops=flops, bytes_accessed=size, transcendentals=0)


def iota(shape, dim):
    return lax.broadcasted_iota(jnp.int32, shape, dim)


def onehot(mask):
    return jnp.where(mask, 1.0, 0.0).astype(BF16)


def dot(a, b, ca=1, cb=0):
    return lax.dot_general(a, b, (((ca,), (cb,)), ((), ())), preferred_element_type=F32)


def softmax_rows(logits):
    raised = jnp.exp(logits)
    return raised / jnp.sum(raised, axis=0, keepdims=True)


def pack_kernel(logits_in, chosen_in, slots_in, rows_in, first_in, out_ref, *scratch):
    held, sems = scratch[:4], scratch[4]
    copies = [
        pltpu.make_async_copy(src, dst, sems.at[k])
        for k, (src, dst) in enumerate(zip((logits_in, chosen_in, slots_in, rows_in), held))
    ]
    for copy in copies:
        copy.start()
    for copy in copies:
        copy.wait()
    logits_ref, chosen_ref, slots_ref, rows_ref = held
    gate = softmax_rows(logits_ref[...]).astype(BF16).astype(F32)
    chosen, slots = chosen_ref[...], slots_ref[...]
    topk, tokens = chosen.shape
    rows = out_ref.shape[0]
    main = jnp.where(slots < 8, chosen * 8 + slots, -1)
    extra = jnp.where((slots >= 8) & (slots < 10), chosen * 2 + slots - 8, -1)
    row = iota((rows, tokens), 0)
    place = jnp.zeros((rows, tokens), F32)
    fold = jnp.zeros((rows, tokens), F32)
    for k in range(topk):
        place = jnp.where(row == main[k : k + 1, :], gate[k : k + 1, :], place)
        fold = jnp.where(row // FOLD == extra[k : k + 1, :], gate[k : k + 1, :], fold)
    place = place.astype(BF16)
    width = rows_ref.shape[1]
    part = width // FOLD
    total = jnp.zeros((rows, part), F32)
    for m in range(FOLD):
        block = rows_ref[:, m * part : (m + 1) * part]
        out_ref[:, m * part : (m + 1) * part] = dot(place, block).astype(BF16)
        total = total + dot(jnp.where(row % FOLD == m, fold, 0.0).astype(BF16), block)
    out_ref[:, width:] = total.astype(BF16)


def permuted_units(core, units, shard):
    half = units // 2
    place = iota((1, units), 1)
    other = (place >= half).astype(jnp.int32)
    inner = place - other * half
    side = jnp.where(other == 1, 1 - core, core)
    block = inner // shard
    return block * (2 * shard) + side * shard + (inner - block * shard)


def hidden_kernel(shard, core_ref, hidden_ref, main_ref, extra_ref, main_t_ref, extra_t_ref):
    rows, units = main_ref.shape
    to_unit = permuted_units(core_ref[0], units, shard)
    column = onehot(iota((units, units), 0) == to_unit)
    source = rows // 8
    here = iota((rows, rows), 0)
    there = iota((rows, rows), 1)
    turn = onehot(there == (here % 8) * source + here // 8)
    turned = dot(turn, hidden_ref[:rows, :]).astype(BF16)
    last = hidden_ref[rows:, :]
    main_ref[...] = dot(turned, column).astype(BF16)
    extra_ref[...] = dot(last, column).astype(BF16)
    main_t_ref[...] = dot(column, turned, 0, 1).astype(BF16)
    extra_t_ref[...] = dot(column, last, 0, 1).astype(BF16)


def unfolded(block, m):
    rows = block.shape[0]
    few = rows // FOLD
    source = rows // 8
    here = iota((few, rows), 0)
    there = iota((few, rows), 1)
    pick = onehot(there == (here % source) * 8 + (here // source) * FOLD + m)
    return dot(pick, block).astype(BF16)


def half_product(main_t_ref, extra_t_ref, rows_ref, fold_ref):
    total = dot(main_t_ref[...], rows_ref[...])
    return total + dot(extra_t_ref[...], unfolded(fold_ref[...], pl.program_id(0)))


def send_kernel(main_t_ref, extra_t_ref, rows_ref, fold_ref, out_ref):
    out_ref[...] = half_product(main_t_ref, extra_t_ref, rows_ref, fold_ref).astype(BF16)


def keep_kernel(main_t_ref, extra_t_ref, rows_ref, fold_ref, arrived_ref, out_ref):
    total = half_product(main_t_ref, extra_t_ref, rows_ref, fold_ref)
    out_ref[...] = (total + arrived_ref[...].astype(F32)).astype(BF16)


def half_partial(main_t, extra_t, payload, half, arrived=None):
    units, rows = main_t.shape
    few = extra_t.shape[1]
    width = payload.shape[1] * FOLD // (FOLD + 1)
    part = width // FOLD
    in_specs = [
        pl.BlockSpec((units // 2, rows), lambda m: (half, 0)),
        pl.BlockSpec((units // 2, few), lambda m: (half, 0)),
        pl.BlockSpec((rows, part), lambda m: (0, m)),
        pl.BlockSpec((rows, part), lambda m: (0, FOLD)),
    ]
    operands = [main_t, extra_t, payload, payload]
    tile = pl.BlockSpec((units // 2, part), lambda m: (0, m))
    if arrived is not None:
        in_specs.append(tile)
        operands.append(arrived)
    return pl.pallas_call(
        send_kernel if arrived is None else keep_kernel,
        grid=(FOLD,),
        in_specs=in_specs,
        out_specs=tile,
        out_shape=pltpu.HBM((units // 2, width), BF16),
        compiler_params=PARAMS,
        cost_estimate=cost(units * (rows + few) * width, 3 * units * width),
        name="half_sent" if arrived is None else "half_kept",
    )(*operands)


def product_kernel(
    shard,
    core_ref,
    main_ref,
    extra_ref,
    own_ref,
    other_ref,
    rows_ref,
    fold_ref,
    grad_ref,
    score_ref,
    acc_main,
    acc_extra,
):
    g = pl.program_id(0)
    rows, units = main_ref.shape
    half = units // 2

    @pl.when(g == 0)
    def _():
        acc_main[...] = jnp.zeros_like(acc_main)
        acc_extra[...] = jnp.zeros_like(acc_extra)

    block = rows_ref[...]
    more = unfolded(fold_ref[...], g)
    for h, weight in enumerate((own_ref[...], other_ref[...])):
        span = slice(h * half, (h + 1) * half)
        acc_main[:, span] += dot(block, weight, 1, 1)
        acc_extra[:, span] += dot(more, weight, 1, 1)

    @pl.when(g == FOLD - 1)
    def _():
        main, extra = acc_main[...], acc_extra[...]
        main_score = jnp.sum(main * main_ref[...].astype(F32), axis=1, keepdims=True)
        extra_score = jnp.sum(extra * extra_ref[...].astype(F32), axis=1, keepdims=True)
        source = rows // 8
        lane = iota((rows, 128), 1)
        spread = jnp.where(lane == iota((rows, 128), 0) % 8, main_score, 0.0)
        scores = jnp.sum(spread.reshape(source, 8, 128), axis=1)
        lane = iota((source, 128), 1)
        for c in range(2):
            scores = jnp.where(lane == 8 + c, extra_score[c * source : (c + 1) * source, :], scores)
        pick = (iota((source, source), 0) ^ core_ref[1]) == iota((source, source), 1)
        score_ref[...] = exact_dot(jnp.where(pick, 1.0, 0.0), scores)
        to_unit = permuted_units(core_ref[0], units, shard)
        column = onehot(iota((units, units), 0) == to_unit)
        here = iota((rows, rows), 0)
        there = iota((rows, rows), 1)
        turn = onehot(there == (here % source) * 8 + here // source)
        turned = dot(turn, main.astype(BF16)).astype(BF16)
        grad_ref[:rows, :] = dot(turned, column, 1, 1).astype(BF16)
        grad_ref[rows:, :] = dot(extra.astype(BF16), column, 1, 1).astype(BF16)


def exact_dot(a, b, ca=1, cb=0):
    return lax.dot_general(
        a,
        b,
        (((ca,), (cb,)), ((), ())),
        precision=lax.Precision.HIGHEST,
        preferred_element_type=F32,
    )


def products(place, shard, main, extra, own, other, payload):
    rows, units = main.shape
    few = rows // FOLD
    width = payload.shape[1] * FOLD // (FOLD + 1)
    part = width // FOLD
    fixed = lambda g: (0, 0)
    moving = lambda g: (0, g)
    return pl.pallas_call(
        functools.partial(product_kernel, shard),
        grid=(FOLD,),
        in_specs=[
            SMEM,
            pl.BlockSpec((rows, units), fixed),
            pl.BlockSpec((few, units), fixed),
            pl.BlockSpec((units // 2, part), moving),
            pl.BlockSpec((units // 2, part), moving),
            pl.BlockSpec((rows, part), moving),
            pl.BlockSpec((rows, part), lambda g: (0, FOLD)),
        ],
        out_specs=[
            pl.BlockSpec((rows + few, units), fixed),
            pl.BlockSpec((rows // 8, 128), fixed),
        ],
        out_shape=[
            jax.ShapeDtypeStruct((rows + few, units), BF16),
            jax.ShapeDtypeStruct((rows // 8, 128), F32),
        ],
        scratch_shapes=[pltpu.VMEM((rows, units), F32), pltpu.VMEM((few, units), F32)],
        compiler_params=PARAMS,
        cost_estimate=cost(0, 0),
        name="products",
    )(place, main, extra, own, other, payload, payload)


def exchanged_by_bits(blocks):
    count, lanes = blocks.shape
    inner = lax.axis_size("x")
    bit = 1
    while bit < count:
        axis, step = ("x", bit) if bit < inner else ("zh", bit // inner)
        size = lax.axis_size(axis)
        pairs = blocks.reshape(count // (2 * bit), 2, bit, lanes)
        came = lax.ppermute(pairs[:, 1], axis, [(i, i ^ step) for i in range(size)])
        blocks = jnp.stack([pairs[:, 0], came], axis=1).reshape(count, lanes)
        bit *= 2
    return blocks


def in_hbm(array):
    return pltpu.with_memory_space_constraint(array, pltpu.HBM)


def after(array, first):
    return pl.pallas_call(
        lambda a, b, c: None,
        in_specs=[HBM, HBM],
        out_specs=HBM,
        out_shape=pltpu.HBM(array.shape, array.dtype),
        input_output_aliases={0: 0},
        cost_estimate=cost(0, 0),
        name="after",
    )(array, first)


def sum_kernel(pieces_ref, out_ref):
    total = pieces_ref[0].astype(F32)
    for k in range(1, pieces_ref.shape[0]):
        total = total + pieces_ref[k].astype(F32)
    out_ref[...] = total


def summed(pieces):
    count, shard, width = pieces.shape
    part = width // 4
    return pl.pallas_call(
        sum_kernel,
        grid=(4,),
        in_specs=[pl.BlockSpec((count, shard, part), lambda g: (0, 0, g))],
        out_specs=pl.BlockSpec((shard, part), lambda g: (0, g)),
        out_shape=jax.ShapeDtypeStruct((shard, width), F32),
        compiler_params=PARAMS,
        cost_estimate=cost(count * shard * width, 2 * count * shard * width),
        name="summed",
    )(pieces)


def logits_kernel(place_ref, logits_ref, chosen_ref, slots_ref, outside_ref, score_ref, out_ref):
    gating = softmax_rows(logits_ref[...])
    sent = gating.astype(BF16).astype(F32)
    chosen, slots = chosen_ref[...], slots_ref[...]
    topk, tokens = chosen.shape
    experts = score_ref.shape[0]
    returned = score_ref[...]
    found = []
    here = chosen ^ place_ref[1]
    for k in range(topk):
        hit = jnp.where(iota((experts, tokens), 0) == here[k : k + 1, :], 1.0, 0.0)
        by_slot = exact_dot(returned, hit, 0, 0)[:16, :]
        at_slot = iota((16, tokens), 0) == slots[k : k + 1, :]
        found.append(jnp.sum(jnp.where(at_slot, by_slot, 0.0), axis=0, keepdims=True))
    inside = jnp.concatenate(found, axis=0) / sent
    outside = jnp.where(chosen >= experts, outside_ref[...], 0.0)
    scores = jnp.where(slots < 10, inside, outside)
    mean = jnp.sum(gating * scores, axis=0, keepdims=True)
    out_ref[...] = gating * (scores - mean)


def body(grad_output, logits, chosen, slots, other_scores, hidden, down_weight):
    tokens, topk = logits.shape
    window, capacity, units = hidden.shape[2], hidden.shape[3], hidden.shape[4]
    model = grad_output.shape[1]
    shard = down_weight.shape[1]
    expert = lax.axis_index(EXPERT)
    place = jnp.stack([lax.axis_index("core"), expert]).astype(jnp.int32)
    logits_t, chosen_t, slots_t = logits.T, chosen.T, slots.T
    swap = [(0, 1), (1, 0)]

    weights = down_weight.reshape(shard, model)
    beside = lax.ppermute(weights, "zl", swap)
    low = lax.axis_index("zl") == 0
    pair = jnp.stack([jnp.where(low, weights, beside), jnp.where(low, beside, weights)])
    own_weights = lax.all_gather(pair, "y").reshape(-1, model)

    packed = pl.pallas_call(
        pack_kernel,
        in_specs=[HBM] * 5,
        out_specs=VMEM,
        out_shape=jax.ShapeDtypeStruct((window * 8, model + model // FOLD), BF16),
        scratch_shapes=[
            pltpu.VMEM((topk, tokens), F32),
            pltpu.VMEM((topk, tokens), jnp.int32),
            pltpu.VMEM((topk, tokens), jnp.int32),
            pltpu.VMEM((tokens, model), BF16),
            pltpu.SemaphoreType.DMA((4,)),
        ],
        compiler_params=PARAMS,
        cost_estimate=cost(2 * 320 * tokens * model * 2, 4 * 320 * model),
        name="pack",
    )(*map(in_hbm, (logits_t, chosen_t, slots_t, grad_output, pair)))
    payload = lax.all_to_all(
        packed.reshape(window, 8, packed.shape[1]), EXPERT, split_axis=0, concat_axis=0, tiled=True
    ).reshape(packed.shape)

    by_slot = hidden.transpose(0, 1, 3, 2, 4).reshape(capacity * window, units)
    main, extra, main_t, extra_t = pl.pallas_call(
        functools.partial(hidden_kernel, shard),
        in_specs=[SMEM, VMEM],
        out_specs=[VMEM] * 4,
        out_shape=[
            jax.ShapeDtypeStruct((window * 8, units), BF16),
            jax.ShapeDtypeStruct((window * 2, units), BF16),
            jax.ShapeDtypeStruct((units, window * 8), BF16),
            jax.ShapeDtypeStruct((units, window * 2), BF16),
        ],
        compiler_params=PARAMS,
        cost_estimate=cost(4 * 320 * units * units, 8 * 320 * units),
        name="hidden_order",
    )(place, by_slot)

    arrived = lax.ppermute(half_partial(main_t, extra_t, payload, 1), "core", swap)
    both = half_partial(main_t, extra_t, payload, 0, arrived)
    pieces = lax.all_to_all(
        both.reshape(-1, shard, model), RING, split_axis=0, concat_axis=0, tiled=True
    )
    grad_down = summed(pieces).reshape(1, shard, model)

    own_weights = after(own_weights, both)
    other_weights = lax.ppermute(own_weights, "core", swap)
    grad, score = products(place, shard, main, extra, own_weights, other_weights, payload)
    grad_hidden = grad.reshape(1, 1, capacity, window, units).transpose(0, 1, 3, 2, 4)
    returned = exchanged_by_bits(score)
    grad_logits = pl.pallas_call(
        logits_kernel,
        in_specs=[SMEM] + [VMEM] * 5,
        out_specs=VMEM,
        out_shape=jax.ShapeDtypeStruct((topk, tokens), F32),
        compiler_params=PARAMS,
        cost_estimate=cost(0, 0),
        name="logits",
    )(place, logits_t, chosen_t, slots_t, other_scores.T, returned)
    return grad_hidden, grad_down, grad_logits.T


def solution(mesh):
    torus = Mesh(mesh.devices.reshape(4, 8, 8, 2, 2), ALL)
    in_specs = (
        P(ALL, None),
        P(ALL, None),
        P(ALL, None),
        P(ALL, None),
        P(ALL, None),
        P(EXPERT, DP, None, None, None),
        P(EXPERT, DP, None),
    )
    out_specs = (P(EXPERT, DP, None, None, None), P(EXPERT, DP, None), P(ALL, None))
    return jax.shard_map(body, mesh=torus, in_specs=in_specs, out_specs=out_specs, check_vma=False)
```

```python
import functools

import jax
import jax.numpy as jnp
from jax import lax
from jax.experimental import pallas as pl
from jax.experimental.pallas import tpu as pltpu
from jax.sharding import Mesh
from jax.sharding import PartitionSpec as P

EXPERT = ("zh", "x")
RING = ("y", "zl")
DP = ("y", "zl", "core")
ALL = EXPERT + DP
FOLD = 4
F32 = jnp.float32
BF16 = jnp.bfloat16
VMEM = pl.BlockSpec(memory_space=pltpu.VMEM)
HBM = pl.BlockSpec(memory_space=pltpu.HBM)
SMEM = pl.BlockSpec(memory_space=pltpu.SMEM)
PARAMS = pltpu.CompilerParams(vmem_limit_bytes=48 * 1024 * 1024)


def cost(flops, size):
    return pl.CostEstimate(flops=flops, bytes_accessed=size, transcendentals=0)


def iota(shape, dim):
    return lax.broadcasted_iota(jnp.int32, shape, dim)


def onehot(mask):
    return jnp.where(mask, 1.0, 0.0).astype(BF16)


def dot(a, b, ca=1, cb=0):
    return lax.dot_general(a, b, (((ca,), (cb,)), ((), ())), preferred_element_type=F32)


def softmax_rows(logits):
    raised = jnp.exp(logits)
    return raised / jnp.sum(raised, axis=0, keepdims=True)


def pack_kernel(logits_in, chosen_in, slots_in, rows_in, out_ref, *scratch):
    held, sems = scratch[:4], scratch[4]
    copies = [
        pltpu.make_async_copy(src, dst, sems.at[k])
        for k, (src, dst) in enumerate(zip((logits_in, chosen_in, slots_in, rows_in), held))
    ]
    for copy in copies:
        copy.start()
    for copy in copies:
        copy.wait()
    logits_ref, chosen_ref, slots_ref, rows_ref = held
    gate = softmax_rows(logits_ref[...]).astype(BF16).astype(F32)
    chosen, slots = chosen_ref[...], slots_ref[...]
    topk, tokens = chosen.shape
    rows = out_ref.shape[0]
    main = jnp.where(slots < 8, chosen * 8 + slots, -1)
    extra = jnp.where((slots >= 8) & (slots < 10), chosen * 2 + slots - 8, -1)
    row = iota((rows, tokens), 0)
    place = jnp.zeros((rows, tokens), F32)
    fold = jnp.zeros((rows, tokens), F32)
    for k in range(topk):
        place = jnp.where(row == main[k : k + 1, :], gate[k : k + 1, :], place)
        fold = jnp.where(row // FOLD == extra[k : k + 1, :], gate[k : k + 1, :], fold)
    place = place.astype(BF16)
    width = rows_ref.shape[1]
    part = width // FOLD
    total = jnp.zeros((rows, part), F32)
    for m in range(FOLD):
        block = rows_ref[:, m * part : (m + 1) * part]
        out_ref[:, m * part : (m + 1) * part] = dot(place, block).astype(BF16)
        total = total + dot(jnp.where(row % FOLD == m, fold, 0.0).astype(BF16), block)
    out_ref[:, width:] = total.astype(BF16)


def permuted_units(core, units, shard):
    half = units // 2
    place = iota((1, units), 1)
    other = (place >= half).astype(jnp.int32)
    inner = place - other * half
    side = jnp.where(other == 1, 1 - core, core)
    block = inner // shard
    return block * (2 * shard) + side * shard + (inner - block * shard)


def hidden_kernel(shard, place_ref, hidden_ref, main_t_ref, extra_t_ref):
    units, rows = main_t_ref.shape
    to_unit = permuted_units(place_ref[0], units, shard)
    column = onehot(iota((units, units), 0) == to_unit)
    source = rows // 8
    here = iota((rows, rows), 0)
    there = iota((rows, rows), 1)
    turn = onehot(there == (here % 8) * source + here // 8)
    turned = dot(turn, hidden_ref[:rows, :]).astype(BF16)
    main_t_ref[...] = dot(column, turned, 0, 1).astype(BF16)
    extra_t_ref[...] = dot(column, hidden_ref[rows:, :], 0, 1).astype(BF16)


def unfolded(block, m):
    rows = block.shape[0]
    few = rows // FOLD
    source = rows // 8
    here = iota((few, rows), 0)
    there = iota((few, rows), 1)
    pick = onehot(there == (here % source) * 8 + (here // source) * FOLD + m)
    return dot(pick, block).astype(BF16)


def half_kernel(half, adds, main_t_ref, extra_t_ref, payload_ref, *refs):
    *given, out_ref, held, sems = refs
    units, width = held.shape
    part = width // FOLD
    span = slice(half * units, (half + 1) * units)
    main_t, extra_t = main_t_ref[span, :], extra_t_ref[span, :]
    fold = payload_ref[:, width:]
    copies = []
    for m in range(FOLD):
        cols = slice(m * part, (m + 1) * part)
        total = dot(main_t, payload_ref[:, cols]) + dot(extra_t, unfolded(fold, m))
        if adds:
            total = total + given[0][:, cols].astype(F32)
        held[:, cols] = total.astype(BF16)
        copies.append(pltpu.make_async_copy(held.at[:, cols], out_ref.at[:, cols], sems.at[m]))
        copies[-1].start()
    for copy in copies:
        copy.wait()


def half_partial(main_t, extra_t, payload, half, arrived=None, first=()):
    given = [] if arrived is None else [arrived]
    units, rows = main_t.shape
    few = extra_t.shape[1]
    width = payload.shape[1] * FOLD // (FOLD + 1)
    return pl.pallas_call(
        functools.partial(half_kernel, half, bool(given)),
        in_specs=[VMEM] * (3 + len(given)) + [HBM] * len(first),
        out_specs=HBM,
        out_shape=pltpu.HBM((units // 2, width), BF16),
        scratch_shapes=[pltpu.VMEM((units // 2, width), BF16), pltpu.SemaphoreType.DMA((FOLD,))],
        compiler_params=PARAMS,
        cost_estimate=cost(units * (rows + few) * width, 3 * units * width),
        name="half_kept" if given else "half_sent",
    )(main_t, extra_t, payload, *given, *map(in_hbm, first))


def product_kernel(
    shard,
    place_ref,
    main_t_ref,
    extra_t_ref,
    own_ref,
    other_ref,
    rows_ref,
    fold_ref,
    grad_ref,
    score_ref,
    acc_main,
    acc_extra,
):
    g = pl.program_id(0)
    units, rows = main_t_ref.shape
    few = extra_t_ref.shape[1]
    half = units // 2
    source = rows // 8

    @pl.when(g == 0)
    def _():
        acc_main[...] = jnp.zeros_like(acc_main)
        acc_extra[...] = jnp.zeros_like(acc_extra)

    block = rows_ref[...]
    more = unfolded(fold_ref[...], g)
    for h, weight in enumerate((own_ref[...], other_ref[...])):
        span = slice(h * half, (h + 1) * half)
        acc_main[span, :] += dot(weight, block, 1, 1)
        acc_extra[span, :] += dot(weight, more, 1, 1)

    @pl.when(g == FOLD - 1)
    def _():
        main, extra = acc_main[...], acc_extra[...]
        main_score = jnp.sum(main * main_t_ref[...].astype(F32), axis=0, keepdims=True)
        extra_score = jnp.sum(extra * extra_t_ref[...].astype(F32), axis=0, keepdims=True)
        to_main = (iota((source, rows), 0) ^ place_ref[1]) == iota((source, rows), 1) // 8
        at_main = iota((rows, 128), 0) % 8 == iota((rows, 128), 1)
        to_extra = (iota((source, few), 0) ^ place_ref[1]) == iota((source, few), 1) % source
        at_extra = iota((few, 128), 0) // source + 8 == iota((few, 128), 1)
        score_ref[...] = exact_dot(
            jnp.where(to_main, main_score, 0.0), jnp.where(at_main, 1.0, 0.0)
        ) + exact_dot(jnp.where(to_extra, extra_score, 0.0), jnp.where(at_extra, 1.0, 0.0))
        to_unit = permuted_units(place_ref[0], units, shard)
        column = onehot(iota((units, units), 0) == to_unit)
        here = iota((rows, rows), 0)
        there = iota((rows, rows), 1)
        turn = onehot(there == (here % source) * 8 + here // source)
        keep = onehot(iota((few, few), 0) == iota((few, few), 1))
        main = dot(column, main.astype(BF16)).astype(BF16)
        extra = dot(column, extra.astype(BF16)).astype(BF16)
        grad_ref[:rows, :] = dot(turn, main, 1, 1).astype(BF16)
        grad_ref[rows:, :] = dot(keep, extra, 1, 1).astype(BF16)


def exact_dot(a, b, ca=1, cb=0):
    return lax.dot_general(
        a,
        b,
        (((ca,), (cb,)), ((), ())),
        precision=lax.Precision.HIGHEST,
        preferred_element_type=F32,
    )


def products(place, shard, main_t, extra_t, own, other, payload):
    units, rows = main_t.shape
    few = extra_t.shape[1]
    width = payload.shape[1] * FOLD // (FOLD + 1)
    part = width // FOLD
    fixed = lambda g: (0, 0)
    moving = lambda g: (0, g)
    return pl.pallas_call(
        functools.partial(product_kernel, shard),
        grid=(FOLD,),
        in_specs=[
            SMEM,
            pl.BlockSpec((units, rows), fixed),
            pl.BlockSpec((units, few), fixed),
            pl.BlockSpec((units // 2, part), moving),
            pl.BlockSpec((units // 2, part), moving),
            pl.BlockSpec((rows, part), moving),
            pl.BlockSpec((rows, part), lambda g: (0, FOLD)),
        ],
        out_specs=[
            pl.BlockSpec((rows + few, units), fixed),
            pl.BlockSpec((rows // 8, 128), fixed),
        ],
        out_shape=[
            jax.ShapeDtypeStruct((rows + few, units), BF16),
            jax.ShapeDtypeStruct((rows // 8, 128), F32),
        ],
        scratch_shapes=[pltpu.VMEM((units, rows), F32), pltpu.VMEM((units, few), F32)],
        compiler_params=PARAMS,
        cost_estimate=cost(0, 0),
        name="products",
    )(place, main_t, extra_t, own, other, payload, payload)


def placed_kernel(place_ref, *refs):
    *pieces, out_ref, sems = refs
    count = len(pieces)
    copies = []
    for k, piece in enumerate(pieces):
        base = lax.rem(place_ref[2] + k, count) * 2
        for t in range(2):
            spot = base + (place_ref[3] ^ t)
            copies.append(pltpu.make_async_copy(piece.at[t], out_ref.at[spot], sems.at[2 * k + t]))
            copies[-1].start()
    for copy in copies:
        copy.wait()


def gathered(place, pair):
    size = lax.axis_size("y")
    down = [(i, (i + size - 1) % size) for i in range(size)]
    up = [(i, (i + 1) % size) for i in range(size)]
    pieces = [pair] + [None] * (size - 1)
    above = below = pair
    for k in range(1, size // 2 + 1):
        above = lax.ppermute(above, "y", down)
        pieces[k] = above
        if k < size - k:
            below = lax.ppermute(below, "y", up)
            pieces[size - k] = below
    shape = (2 * size, *pair.shape[1:])
    return pl.pallas_call(
        placed_kernel,
        in_specs=[SMEM] + [HBM] * size,
        out_specs=HBM,
        out_shape=pltpu.HBM(shape, pair.dtype),
        scratch_shapes=[pltpu.SemaphoreType.DMA((2 * size,))],
        cost_estimate=cost(0, 0),
        name="placed",
    )(place, *pieces), pieces


def pair_kernel(weights_ref, beside_ref, out_ref, sems):
    copies = [
        pltpu.make_async_copy(src, out_ref.at[k], sems.at[k])
        for k, src in enumerate((weights_ref, beside_ref))
    ]
    for copy in copies:
        copy.start()
    for copy in copies:
        copy.wait()


def paired(weights, beside):
    return pl.pallas_call(
        pair_kernel,
        in_specs=[HBM] * 2,
        out_specs=HBM,
        out_shape=pltpu.HBM((2, *weights.shape), weights.dtype),
        scratch_shapes=[pltpu.SemaphoreType.DMA((2,))],
        cost_estimate=cost(0, 0),
        name="paired",
    )(weights, beside)


def exchanged_by_bits(blocks):
    count, lanes = blocks.shape
    inner = lax.axis_size("x")
    bit = 1
    while bit < count:
        axis, step = ("x", bit) if bit < inner else ("zh", bit // inner)
        size = lax.axis_size(axis)
        pairs = blocks.reshape(count // (2 * bit), 2, bit, lanes)
        came = lax.ppermute(pairs[:, 1], axis, [(i, i ^ step) for i in range(size)])
        blocks = jnp.stack([pairs[:, 0], came], axis=1).reshape(count, lanes)
        bit *= 2
    return blocks


def in_hbm(array):
    return pltpu.with_memory_space_constraint(array, pltpu.HBM)


def after_kernel(array_ref, first_ref, out_ref, sem):
    copy = pltpu.make_async_copy(array_ref, out_ref, sem)
    copy.start()
    copy.wait()


def after(array, first):
    return pl.pallas_call(
        after_kernel,
        in_specs=[HBM, HBM],
        out_specs=HBM,
        out_shape=pltpu.HBM(array.shape, array.dtype),
        scratch_shapes=[pltpu.SemaphoreType.DMA],
        cost_estimate=cost(0, 0),
        name="after",
    )(array, first)


def sum_kernel(pieces_ref, out_ref):
    total = pieces_ref[0].astype(F32)
    for k in range(1, pieces_ref.shape[0]):
        total = total + pieces_ref[k].astype(F32)
    out_ref[...] = total


def summed(pieces):
    count, shard, width = pieces.shape
    part = width // 4
    return pl.pallas_call(
        sum_kernel,
        grid=(4,),
        in_specs=[pl.BlockSpec((count, shard, part), lambda g: (0, 0, g))],
        out_specs=pl.BlockSpec((shard, part), lambda g: (0, g)),
        out_shape=jax.ShapeDtypeStruct((shard, width), F32),
        compiler_params=PARAMS,
        cost_estimate=cost(count * shard * width, 2 * count * shard * width),
        name="summed",
    )(pieces)


def logits_kernel(place_ref, logits_ref, chosen_ref, slots_ref, outside_ref, score_ref, out_ref):
    gating = softmax_rows(logits_ref[...])
    sent = gating.astype(BF16).astype(F32)
    chosen, slots = chosen_ref[...], slots_ref[...]
    topk, tokens = chosen.shape
    experts = score_ref.shape[0]
    returned = score_ref[...]
    found = []
    here = chosen ^ place_ref[1]
    for k in range(topk):
        hit = jnp.where(iota((experts, tokens), 0) == here[k : k + 1, :], 1.0, 0.0)
        by_slot = exact_dot(returned, hit, 0, 0)[:16, :]
        at_slot = iota((16, tokens), 0) == slots[k : k + 1, :]
        found.append(jnp.sum(jnp.where(at_slot, by_slot, 0.0), axis=0, keepdims=True))
    inside = jnp.concatenate(found, axis=0) / sent
    outside = jnp.where(chosen >= experts, outside_ref[...], 0.0)
    scores = jnp.where(slots < 10, inside, outside)
    mean = jnp.sum(gating * scores, axis=0, keepdims=True)
    out_ref[...] = gating * (scores - mean)


def body(grad_output, logits, chosen, slots, other_scores, hidden, down_weight):
    tokens, topk = logits.shape
    window, capacity, units = hidden.shape[2], hidden.shape[3], hidden.shape[4]
    model = grad_output.shape[1]
    shard = down_weight.shape[1]
    expert = lax.axis_index(EXPERT)
    place = [lax.axis_index("core"), expert, lax.axis_index("y"), lax.axis_index("zl")]
    place = jnp.stack(place).astype(jnp.int32)
    logits_t, chosen_t, slots_t = logits.T, chosen.T, slots.T
    swap = [(0, 1), (1, 0)]

    packed = pl.pallas_call(
        pack_kernel,
        in_specs=[HBM] * 4,
        out_specs=VMEM,
        out_shape=jax.ShapeDtypeStruct((window * 8, model + model // FOLD), BF16),
        scratch_shapes=[
            pltpu.VMEM((topk, tokens), F32),
            pltpu.VMEM((topk, tokens), jnp.int32),
            pltpu.VMEM((topk, tokens), jnp.int32),
            pltpu.VMEM((tokens, model), BF16),
            pltpu.SemaphoreType.DMA((4,)),
        ],
        compiler_params=PARAMS,
        cost_estimate=cost(2 * 320 * tokens * model * 2, 4 * 320 * model),
        name="pack",
    )(*map(in_hbm, (logits_t, chosen_t, slots_t, grad_output)))
    payload = lax.all_to_all(
        packed.reshape(window, 8, packed.shape[1]), EXPERT, split_axis=0, concat_axis=0, tiled=True
    ).reshape(packed.shape)

    weights = after(down_weight.reshape(shard, model), packed)
    beside = lax.ppermute(weights, "zl", swap)
    own_weights, pieces = gathered(place, paired(weights, beside))
    own_weights = own_weights.reshape(-1, model)
    other_weights = lax.ppermute(own_weights, "core", swap)

    by_slot = hidden.transpose(0, 1, 3, 2, 4).reshape(capacity * window, units)
    main_t, extra_t = pl.pallas_call(
        functools.partial(hidden_kernel, shard),
        in_specs=[SMEM, VMEM],
        out_specs=[VMEM] * 2,
        out_shape=[
            jax.ShapeDtypeStruct((units, window * 8), BF16),
            jax.ShapeDtypeStruct((units, window * 2), BF16),
        ],
        compiler_params=PARAMS,
        cost_estimate=cost(4 * 320 * units * units, 8 * 320 * units),
        name="hidden_order",
    )(place, by_slot)

    sent = half_partial(main_t, extra_t, payload, 1, first=(pieces[3], pieces[-3]))
    arrived = lax.ppermute(sent, "core", swap)
    both = half_partial(main_t, extra_t, payload, 0, arrived)
    pieces = lax.all_to_all(
        both.reshape(-1, shard, model), RING, split_axis=0, concat_axis=0, tiled=True
    )
    grad_down = summed(pieces).reshape(1, shard, model)

    grad, score = products(place, shard, main_t, extra_t, own_weights, other_weights, payload)
    grad_hidden = grad.reshape(1, 1, capacity, window, units).transpose(0, 1, 3, 2, 4)
    returned = exchanged_by_bits(score)
    grad_logits = pl.pallas_call(
        logits_kernel,
        in_specs=[SMEM] + [VMEM] * 5,
        out_specs=VMEM,
        out_shape=jax.ShapeDtypeStruct((topk, tokens), F32),
        compiler_params=PARAMS,
        cost_estimate=cost(0, 0),
        name="logits",
    )(place, logits_t, chosen_t, slots_t, other_scores.T, returned)
    return grad_hidden, grad_down, grad_logits.T


def solution(mesh):
    torus = Mesh(mesh.devices.reshape(4, 8, 8, 2, 2), ALL)
    in_specs = (
        P(ALL, None),
        P(ALL, None),
        P(ALL, None),
        P(ALL, None),
        P(ALL, None),
        P(EXPERT, DP, None, None, None),
        P(EXPERT, DP, None),
    )
    out_specs = (P(EXPERT, DP, None, None, None), P(EXPERT, DP, None), P(ALL, None))
    return jax.shard_map(body, mesh=torus, in_specs=in_specs, out_specs=out_specs, check_vma=False)
```

```python
import functools

import jax
import jax.numpy as jnp
from jax import lax
from jax.experimental import pallas as pl
from jax.experimental.pallas import tpu as pltpu
from jax.sharding import Mesh
from jax.sharding import PartitionSpec as P

EXPERT = ("zh", "x")
RING = ("y", "zl")
DP = ("y", "zl", "core")
ALL = EXPERT + DP
FOLD = 4
F32 = jnp.float32
BF16 = jnp.bfloat16
VMEM = pl.BlockSpec(memory_space=pltpu.VMEM)
HBM = pl.BlockSpec(memory_space=pltpu.HBM)
ANY = pl.BlockSpec(memory_space=pl.ANY)
SMEM = pl.BlockSpec(memory_space=pltpu.SMEM)
PARAMS = pltpu.CompilerParams(vmem_limit_bytes=48 * 1024 * 1024)


def cost(flops, size):
    return pl.CostEstimate(flops=flops, bytes_accessed=size, transcendentals=0)


def iota(shape, dim):
    return lax.broadcasted_iota(jnp.int32, shape, dim)


def onehot(mask):
    return jnp.where(mask, 1.0, 0.0).astype(BF16)


def dot(a, b, ca=1, cb=0):
    return lax.dot_general(a, b, (((ca,), (cb,)), ((), ())), preferred_element_type=F32)


def softmax_rows(logits):
    raised = jnp.exp(logits)
    return raised / jnp.sum(raised, axis=0, keepdims=True)


def place_kernel(logits_in, chosen_in, slots_in, place_ref, fold_ref, *scratch):
    held, sems = scratch[:3], scratch[3]
    copies = [
        pltpu.make_async_copy(src, dst, sems.at[k])
        for k, (src, dst) in enumerate(zip((logits_in, chosen_in, slots_in), held))
    ]
    for copy in copies:
        copy.start()
    for copy in copies:
        copy.wait()
    logits_ref, chosen_ref, slots_ref = held
    gate = softmax_rows(logits_ref[...]).astype(BF16).astype(F32)
    chosen, slots = chosen_ref[...], slots_ref[...]
    topk, tokens = chosen.shape
    rows = place_ref.shape[0]
    main = jnp.where(slots < 8, chosen * 8 + slots, -1)
    extra = jnp.where((slots >= 8) & (slots < 10), chosen * 2 + slots - 8, -1)
    row = iota((rows, tokens), 0)
    place = jnp.zeros((rows, tokens), F32)
    fold = jnp.zeros((rows, tokens), F32)
    for k in range(topk):
        place = jnp.where(row == main[k : k + 1, :], gate[k : k + 1, :], place)
        fold = jnp.where(row // FOLD == extra[k : k + 1, :], gate[k : k + 1, :], fold)
    place_ref[...] = place.astype(BF16)
    fold_ref[...] = fold.astype(BF16)


def pack_kernel(place_ref, fold_ref, rows_in, first_in, out_ref, rows_ref, sem):
    copy = pltpu.make_async_copy(rows_in, rows_ref, sem)
    copy.start()
    copy.wait()
    place, fold = place_ref[...], fold_ref[...].astype(F32)
    rows, tokens = place.shape
    row = iota((rows, tokens), 0)
    width = rows_ref.shape[1]
    part = width // FOLD
    total = jnp.zeros((rows, part), F32)
    for m in range(FOLD):
        block = rows_ref[:, m * part : (m + 1) * part]
        out_ref[:, m * part : (m + 1) * part] = dot(place, block).astype(BF16)
        total = total + dot(jnp.where(row % FOLD == m, fold, 0.0).astype(BF16), block)
    out_ref[:, width:] = total.astype(BF16)


def permuted_units(core, units, shard):
    half = units // 2
    place = iota((1, units), 1)
    other = (place >= half).astype(jnp.int32)
    inner = place - other * half
    side = jnp.where(other == 1, 1 - core, core)
    block = inner // shard
    return block * (2 * shard) + side * shard + (inner - block * shard)


def hidden_kernel(shard, place_ref, hidden_ref, main_t_ref, extra_t_ref):
    units, rows = main_t_ref.shape
    to_unit = permuted_units(place_ref[0], units, shard)
    column = onehot(iota((units, units), 0) == to_unit)
    source = rows // 8
    here = iota((rows, rows), 0)
    there = iota((rows, rows), 1)
    turn = onehot(there == (here % 8) * source + here // 8)
    turned = dot(turn, hidden_ref[:rows, :]).astype(BF16)
    main_t_ref[...] = dot(column, turned, 0, 1).astype(BF16)
    extra_t_ref[...] = dot(column, hidden_ref[rows:, :], 0, 1).astype(BF16)


def unfolded(block, m):
    rows = block.shape[0]
    few = rows // FOLD
    source = rows // 8
    here = iota((few, rows), 0)
    there = iota((few, rows), 1)
    pick = onehot(there == (here % source) * 8 + (here // source) * FOLD + m)
    return dot(pick, block).astype(BF16)


def half_kernel(half, adds, main_t_ref, extra_t_ref, payload_ref, *refs):
    *given, out_ref, held, sems = refs
    units, width = held.shape
    part = width // FOLD
    span = slice(half * units, (half + 1) * units)
    main_t, extra_t = main_t_ref[span, :], extra_t_ref[span, :]
    fold = payload_ref[:, width:]
    copies = []
    for m in range(FOLD):
        cols = slice(m * part, (m + 1) * part)
        total = dot(main_t, payload_ref[:, cols]) + dot(extra_t, unfolded(fold, m))
        if adds:
            total = total + given[0][:, cols].astype(F32)
        held[:, cols] = total.astype(BF16)
        copies.append(pltpu.make_async_copy(held.at[:, cols], out_ref.at[:, cols], sems.at[m]))
        copies[-1].start()
    for copy in copies:
        copy.wait()


def half_partial(main_t, extra_t, payload, half, arrived=None, first=()):
    given = [] if arrived is None else [arrived]
    units, rows = main_t.shape
    few = extra_t.shape[1]
    width = payload.shape[1] * FOLD // (FOLD + 1)
    return pl.pallas_call(
        functools.partial(half_kernel, half, bool(given)),
        in_specs=[VMEM] * (3 + len(given)) + [ANY] * len(first),
        out_specs=HBM,
        out_shape=pltpu.HBM((units // 2, width), BF16),
        scratch_shapes=[pltpu.VMEM((units // 2, width), BF16), pltpu.SemaphoreType.DMA((FOLD,))],
        compiler_params=PARAMS,
        cost_estimate=cost(units * (rows + few) * width, 3 * units * width),
        name="half_kept" if given else "half_sent",
    )(main_t, extra_t, payload, *given, *first)


def product_kernel(half, place_ref, main_t_ref, extra_t_ref, weights_ref, payload_ref, *refs):
    *given, main_ref, extra_ref, score_ref = refs
    units, rows = main_ref.shape
    few = extra_ref.shape[1]
    source = rows // 8
    width = weights_ref.shape[1]
    part = width // FOLD
    weights = weights_ref[...]
    fold = payload_ref[:, width:]
    main = dot(weights, payload_ref[:, :width], 1, 1)
    extra = jnp.zeros((units, few), F32)
    for m in range(FOLD):
        extra = extra + dot(weights[:, m * part : (m + 1) * part], unfolded(fold, m), 1, 1)
    main_ref[...] = main.astype(BF16)
    extra_ref[...] = extra.astype(BF16)
    span = slice(half * units, (half + 1) * units)
    main_score = jnp.sum(main * main_t_ref[span, :].astype(F32), axis=0, keepdims=True)
    extra_score = jnp.sum(extra * extra_t_ref[span, :].astype(F32), axis=0, keepdims=True)
    to_main = (iota((source, rows), 0) ^ place_ref[1]) == iota((source, rows), 1) // 8
    at_main = iota((rows, 128), 0) % 8 == iota((rows, 128), 1)
    to_extra = (iota((source, few), 0) ^ place_ref[1]) == iota((source, few), 1) % source
    at_extra = iota((few, 128), 0) // source + 8 == iota((few, 128), 1)
    score = exact_dot(jnp.where(to_main, main_score, 0.0), jnp.where(at_main, 1.0, 0.0))
    score = score + exact_dot(jnp.where(to_extra, extra_score, 0.0), jnp.where(at_extra, 1.0, 0.0))
    if given:
        score = score + given[0][...]
    score_ref[...] = score


def half_product(place, main_t, extra_t, weights, payload, half, *given):
    units, rows = main_t.shape
    few = extra_t.shape[1]
    return pl.pallas_call(
        functools.partial(product_kernel, half),
        in_specs=[SMEM] + [VMEM] * (4 + len(given)),
        out_specs=[VMEM] * 3,
        out_shape=[
            jax.ShapeDtypeStruct((units // 2, rows), BF16),
            jax.ShapeDtypeStruct((units // 2, few), BF16),
            jax.ShapeDtypeStruct((rows // 8, 128), F32),
        ],
        compiler_params=PARAMS,
        cost_estimate=cost(units * (rows + few) * weights.shape[1], 0),
        name="product_of_other" if half else "product_of_own",
    )(place, main_t, extra_t, weights, payload, *given)


def order_kernel(shard, place_ref, own_main, own_extra, other_main, other_extra, grad_ref):
    half, rows = own_main.shape
    few = own_extra.shape[1]
    units = 2 * half
    source = rows // 8
    to_unit = permuted_units(place_ref[0], units, shard)
    column = onehot(iota((units, units), 0) == to_unit)
    here = iota((rows, rows), 0)
    turn = onehot(iota((rows, rows), 1) == (here % source) * 8 + here // source)
    keep = onehot(iota((few, few), 0) == iota((few, few), 1))
    own, other = column[:, :half], column[:, half:]
    main = (dot(own, own_main[...]) + dot(other, other_main[...])).astype(BF16)
    extra = (dot(own, own_extra[...]) + dot(other, other_extra[...])).astype(BF16)
    grad_ref[:rows, :] = dot(turn, main, 1, 1).astype(BF16)
    grad_ref[rows:, :] = dot(keep, extra, 1, 1).astype(BF16)


def exact_dot(a, b, ca=1, cb=0):
    return lax.dot_general(
        a,
        b,
        (((ca,), (cb,)), ((), ())),
        precision=lax.Precision.HIGHEST,
        preferred_element_type=F32,
    )


def placed_kernel(place_ref, *refs):
    *pieces, out_ref = refs
    count = len(pieces)
    for k, piece in enumerate(pieces):
        base = lax.rem(place_ref[2] + k, count) * 2
        for t in range(2):
            out_ref[base + (place_ref[3] ^ t)] = piece[t]


def gathered(place, pair):
    size = lax.axis_size("y")
    down = [(i, (i + size - 1) % size) for i in range(size)]
    up = [(i, (i + 1) % size) for i in range(size)]
    pieces = [pair] + [None] * (size - 1)
    above = below = pair
    for k in range(1, size // 2 + 1):
        above = lax.ppermute(above, "y", down)
        pieces[k] = above
        if k < size - k:
            below = lax.ppermute(below, "y", up)
            pieces[size - k] = below
    placed = pl.pallas_call(
        placed_kernel,
        in_specs=[SMEM] + [VMEM] * size,
        out_specs=VMEM,
        out_shape=jax.ShapeDtypeStruct((2 * size, *pair.shape[1:]), pair.dtype),
        compiler_params=PARAMS,
        cost_estimate=cost(0, 0),
        name="placed",
    )(place, *pieces)
    return placed, pieces


def pair_kernel(weights_ref, beside_ref, first_ref, out_ref):
    out_ref[0] = weights_ref[...]
    out_ref[1] = beside_ref[...]


def paired(weights, beside, first):
    return pl.pallas_call(
        pair_kernel,
        in_specs=[VMEM, VMEM, ANY],
        out_specs=VMEM,
        out_shape=jax.ShapeDtypeStruct((2, *weights.shape), weights.dtype),
        compiler_params=PARAMS,
        cost_estimate=cost(0, 0),
        name="paired",
    )(weights, beside, first)


def exchanged_by_bits(blocks):
    count, lanes = blocks.shape
    inner = lax.axis_size("x")
    bit = 1
    while bit < count:
        axis, step = ("x", bit) if bit < inner else ("zh", bit // inner)
        size = lax.axis_size(axis)
        pairs = blocks.reshape(count // (2 * bit), 2, bit, lanes)
        came = lax.ppermute(pairs[:, 1], axis, [(i, i ^ step) for i in range(size)])
        blocks = jnp.stack([pairs[:, 0], came], axis=1).reshape(count, lanes)
        bit *= 2
    return blocks


def in_hbm(array):
    return pltpu.with_memory_space_constraint(array, pltpu.HBM)


def sum_kernel(pieces_ref, out_ref):
    total = pieces_ref[0].astype(F32)
    for k in range(1, pieces_ref.shape[0]):
        total = total + pieces_ref[k].astype(F32)
    out_ref[...] = total


def summed(pieces):
    count, shard, width = pieces.shape
    part = width // 4
    return pl.pallas_call(
        sum_kernel,
        grid=(4,),
        in_specs=[pl.BlockSpec((count, shard, part), lambda g: (0, 0, g))],
        out_specs=pl.BlockSpec((shard, part), lambda g: (0, g)),
        out_shape=jax.ShapeDtypeStruct((shard, width), F32),
        compiler_params=PARAMS,
        cost_estimate=cost(count * shard * width, 2 * count * shard * width),
        name="summed",
    )(pieces)


def logits_kernel(place_ref, logits_ref, chosen_ref, slots_ref, outside_ref, score_ref, out_ref):
    gating = softmax_rows(logits_ref[...])
    sent = gating.astype(BF16).astype(F32)
    chosen, slots = chosen_ref[...], slots_ref[...]
    topk, tokens = chosen.shape
    experts = score_ref.shape[0]
    returned = score_ref[...]
    found = []
    here = chosen ^ place_ref[1]
    for k in range(topk):
        hit = jnp.where(iota((experts, tokens), 0) == here[k : k + 1, :], 1.0, 0.0)
        by_slot = exact_dot(returned, hit, 0, 0)[:16, :]
        at_slot = iota((16, tokens), 0) == slots[k : k + 1, :]
        found.append(jnp.sum(jnp.where(at_slot, by_slot, 0.0), axis=0, keepdims=True))
    inside = jnp.concatenate(found, axis=0) / sent
    outside = jnp.where(chosen >= experts, outside_ref[...], 0.0)
    scores = jnp.where(slots < 10, inside, outside)
    mean = jnp.sum(gating * scores, axis=0, keepdims=True)
    out_ref[...] = gating * (scores - mean)


def body(grad_output, logits, chosen, slots, other_scores, hidden, down_weight):
    tokens, topk = logits.shape
    window, capacity, units = hidden.shape[2], hidden.shape[3], hidden.shape[4]
    model = grad_output.shape[1]
    shard = down_weight.shape[1]
    expert = lax.axis_index(EXPERT)
    place = [lax.axis_index("core"), expert, lax.axis_index("y"), lax.axis_index("zl")]
    place = jnp.stack(place).astype(jnp.int32)
    logits_t, chosen_t, slots_t = logits.T, chosen.T, slots.T
    swap = [(0, 1), (1, 0)]

    weights = down_weight.reshape(shard, model)
    beside = lax.ppermute(weights, "zl", swap)
    tile = jax.ShapeDtypeStruct((window * 8, tokens), BF16)
    placing = pl.pallas_call(
        place_kernel,
        in_specs=[HBM] * 3,
        out_specs=[VMEM] * 2,
        out_shape=[tile, tile],
        scratch_shapes=[
            pltpu.VMEM((topk, tokens), F32),
            pltpu.VMEM((topk, tokens), jnp.int32),
            pltpu.VMEM((topk, tokens), jnp.int32),
            pltpu.SemaphoreType.DMA((3,)),
        ],
        compiler_params=PARAMS,
        cost_estimate=cost(0, 4 * 320 * model),
        name="placing",
    )(*map(in_hbm, (logits_t, chosen_t, slots_t)))
    packed = pl.pallas_call(
        pack_kernel,
        in_specs=[VMEM, VMEM, HBM, ANY],
        out_specs=VMEM,
        out_shape=jax.ShapeDtypeStruct((window * 8, model + model // FOLD), BF16),
        scratch_shapes=[pltpu.VMEM((tokens, model), BF16), pltpu.SemaphoreType.DMA],
        compiler_params=PARAMS,
        cost_estimate=cost(2 * 320 * tokens * model * 2, 4 * 320 * model),
        name="pack",
    )(*placing, in_hbm(grad_output), beside)
    payload = lax.all_to_all(
        packed.reshape(window, 8, packed.shape[1]), EXPERT, split_axis=0, concat_axis=0, tiled=True
    ).reshape(packed.shape)

    own_weights, pieces = gathered(place, paired(weights, beside, packed))
    own_weights = own_weights.reshape(-1, model)
    other_weights = lax.ppermute(own_weights, "core", swap)

    by_slot = hidden.transpose(0, 1, 3, 2, 4).reshape(capacity * window, units)
    main_t, extra_t = pl.pallas_call(
        functools.partial(hidden_kernel, shard),
        in_specs=[SMEM, VMEM],
        out_specs=[VMEM] * 2,
        out_shape=[
            jax.ShapeDtypeStruct((units, window * 8), BF16),
            jax.ShapeDtypeStruct((units, window * 2), BF16),
        ],
        compiler_params=PARAMS,
        cost_estimate=cost(4 * 320 * units * units, 8 * 320 * units),
        name="hidden_order",
    )(place, by_slot)

    sent = half_partial(main_t, extra_t, payload, 1, first=(pieces[3], pieces[-3]))
    arrived = lax.ppermute(sent, "core", swap)
    both = half_partial(main_t, extra_t, payload, 0, arrived)
    parts = lax.all_to_all(
        both.reshape(-1, shard, model), RING, split_axis=0, concat_axis=0, tiled=True
    )
    grad_down = summed(parts).reshape(1, shard, model)

    *own_grad, score = half_product(place, main_t, extra_t, own_weights, payload, 0)
    *other_grad, score = half_product(place, main_t, extra_t, other_weights, payload, 1, score)
    returned = exchanged_by_bits(score)
    grad = pl.pallas_call(
        functools.partial(order_kernel, shard),
        in_specs=[SMEM] + [VMEM] * 4,
        out_specs=VMEM,
        out_shape=jax.ShapeDtypeStruct((capacity * window, units), BF16),
        compiler_params=PARAMS,
        cost_estimate=cost(2 * 320 * units * units, 4 * 320 * units),
        name="order",
    )(place, *own_grad, *other_grad)
    grad_hidden = grad.reshape(1, 1, capacity, window, units).transpose(0, 1, 3, 2, 4)
    grad_logits = pl.pallas_call(
        logits_kernel,
        in_specs=[SMEM] + [VMEM] * 5,
        out_specs=VMEM,
        out_shape=jax.ShapeDtypeStruct((topk, tokens), F32),
        compiler_params=PARAMS,
        cost_estimate=cost(0, 0),
        name="logits",
    )(place, logits_t, chosen_t, slots_t, other_scores.T, returned)
    return grad_hidden, grad_down, grad_logits.T


def solution(mesh):
    torus = Mesh(mesh.devices.reshape(4, 8, 8, 2, 2), ALL)
    in_specs = (
        P(ALL, None),
        P(ALL, None),
        P(ALL, None),
        P(ALL, None),
        P(ALL, None),
        P(EXPERT, DP, None, None, None),
        P(EXPERT, DP, None),
    )
    out_specs = (P(EXPERT, DP, None, None, None), P(EXPERT, DP, None), P(ALL, None))
    return jax.shard_map(body, mesh=torus, in_specs=in_specs, out_specs=out_specs, check_vma=False)
```

```python
import functools

import jax
import jax.numpy as jnp
from jax import lax
from jax.experimental import pallas as pl
from jax.experimental.pallas import tpu as pltpu
from jax.sharding import Mesh
from jax.sharding import PartitionSpec as P

EXPERT = ("zh", "x")
RING = ("y", "zl")
DP = ("y", "zl", "core")
ALL = EXPERT + DP
FOLD = 4
F32 = jnp.float32
BF16 = jnp.bfloat16
VMEM = pl.BlockSpec(memory_space=pltpu.VMEM)
HBM = pl.BlockSpec(memory_space=pltpu.HBM)
SMEM = pl.BlockSpec(memory_space=pltpu.SMEM)
PARAMS = pltpu.CompilerParams(vmem_limit_bytes=12 * 1024 * 1024)


def cost(flops, size):
    return pl.CostEstimate(flops=flops, bytes_accessed=size, transcendentals=0)


def iota(shape, dim):
    return lax.broadcasted_iota(jnp.int32, shape, dim)


def onehot(mask):
    return jnp.where(mask, 1.0, 0.0).astype(BF16)


def dot(a, b, ca=1, cb=0):
    return lax.dot_general(a, b, (((ca,), (cb,)), ((), ())), preferred_element_type=F32)


def softmax_rows(logits):
    raised = jnp.exp(logits)
    return raised / jnp.sum(raised, axis=0, keepdims=True)


def place_kernel(logits_in, chosen_in, slots_in, place_ref, fold_ref, *scratch):
    held, sems = scratch[:3], scratch[3]
    copies = [
        pltpu.make_async_copy(src, dst, sems.at[k])
        for k, (src, dst) in enumerate(zip((logits_in, chosen_in, slots_in), held))
    ]
    for copy in copies:
        copy.start()
    for copy in copies:
        copy.wait()
    logits_ref, chosen_ref, slots_ref = held
    gate = softmax_rows(logits_ref[...]).astype(BF16).astype(F32)
    chosen, slots = chosen_ref[...], slots_ref[...]
    topk, tokens = chosen.shape
    rows = place_ref.shape[0]
    main = jnp.where(slots < 8, chosen * 8 + slots, -1)
    extra = jnp.where((slots >= 8) & (slots < 10), chosen * 2 + slots - 8, -1)
    row = iota((rows, tokens), 0)
    place = jnp.zeros((rows, tokens), F32)
    fold = jnp.zeros((rows, tokens), F32)
    for k in range(topk):
        place = jnp.where(row == main[k : k + 1, :], gate[k : k + 1, :], place)
        fold = jnp.where(row // FOLD == extra[k : k + 1, :], gate[k : k + 1, :], fold)
    place_ref[...] = place.astype(BF16)
    fold_ref[...] = fold.astype(BF16)


def pack_kernel(place_ref, fold_ref, rows_in, out_ref, rows_ref, held, sems):
    copy = pltpu.make_async_copy(rows_in, rows_ref, sems.at[0])
    copy.start()
    place, fold = place_ref[...], fold_ref[...].astype(F32)
    rows, tokens = place.shape
    row = iota((rows, tokens), 0)
    folds = [jnp.where(row % FOLD == m, fold, 0.0).astype(BF16) for m in range(FOLD)]
    part = rows_ref.shape[1] // FOLD
    total = jnp.zeros((rows, part), F32)
    copy.wait()
    copies = []
    for m in range(FOLD + 1):
        cols = slice(m * part, (m + 1) * part)
        if m < FOLD:
            block = rows_ref[:, cols]
            held[:, cols] = dot(place, block).astype(BF16)
            total = total + dot(folds[m], block)
        else:
            held[:, cols] = total.astype(BF16)
        copies.append(pltpu.make_async_copy(held.at[:, cols], out_ref.at[:, cols], sems.at[m + 1]))
        copies[-1].start()
    for copy in copies:
        copy.wait()


def permuted_units(core, units, shard):
    half = units // 2
    place = iota((1, units), 1)
    other = (place >= half).astype(jnp.int32)
    inner = place - other * half
    side = jnp.where(other == 1, 1 - core, core)
    block = inner // shard
    return block * (2 * shard) + side * shard + (inner - block * shard)


def hidden_kernel(shard, place_ref, hidden_ref, main_t_ref, extra_t_ref):
    units, rows = main_t_ref.shape
    to_unit = permuted_units(place_ref[0], units, shard)
    column = onehot(iota((units, units), 0) == to_unit)
    source = rows // 8
    here = iota((rows, rows), 0)
    there = iota((rows, rows), 1)
    turn = onehot(there == (here % 8) * source + here // 8)
    turned = dot(turn, hidden_ref[:rows, :]).astype(BF16)
    main_t_ref[...] = dot(column, turned, 0, 1).astype(BF16)
    extra_t_ref[...] = dot(column, hidden_ref[rows:, :], 0, 1).astype(BF16)


def unfolded(block, m):
    rows = block.shape[0]
    few = rows // FOLD
    source = rows // 8
    here = iota((few, rows), 0)
    there = iota((few, rows), 1)
    pick = onehot(there == (here % source) * 8 + (here // source) * FOLD + m)
    return dot(pick, block).astype(BF16)


def columns(m, part):
    return pl.ds(pl.multiple_of(m * part, part), part)


def half_kernel(half, adds, main_t_ref, extra_t_ref, payload_ref, *refs):
    *given, out_ref, held, sems = refs
    units, width = held.shape
    part = width // FOLD
    span = slice(half * units, (half + 1) * units)

    def copy_of(m):
        cols = columns(m, part)
        return pltpu.make_async_copy(held.at[:, cols], out_ref.at[:, cols], sems.at[m])

    def step(m, carry):
        cols = columns(m, part)
        total = dot(main_t_ref[span, :], payload_ref[:, cols])
        total = total + dot(extra_t_ref[span, :], unfolded(payload_ref[:, width:], m))
        if adds:
            total = total + given[0][:, cols].astype(F32)
        held[:, cols] = total.astype(BF16)
        copy_of(m).start()
        return carry

    def wait(m, carry):
        copy_of(m).wait()
        return carry

    lax.fori_loop(0, FOLD, step, 0)
    lax.fori_loop(0, FOLD, wait, 0)


def half_partial(main_t, extra_t, payload, half, arrived=None, first=()):
    given = [] if arrived is None else [arrived]
    units, rows = main_t.shape
    few = extra_t.shape[1]
    width = payload.shape[1] * FOLD // (FOLD + 1)
    return pl.pallas_call(
        functools.partial(half_kernel, half, bool(given)),
        in_specs=[VMEM] * (3 + len(given)) + [VMEM] * len(first),
        out_specs=HBM,
        out_shape=pltpu.HBM((units // 2, width), BF16),
        scratch_shapes=[pltpu.VMEM((units // 2, width), BF16), pltpu.SemaphoreType.DMA((FOLD,))],
        compiler_params=PARAMS,
        cost_estimate=cost(units * (rows + few) * width, 3 * units * width),
        name="half_kept" if given else "half_sent",
    )(main_t, extra_t, payload, *given, *first)


def product_kernel(half, main_t_ref, extra_t_ref, weights_ref, payload_ref, *refs):
    *given, main_ref, extra_ref, score_ref, acc_main, acc_extra = refs
    units, rows = main_ref.shape
    few = extra_ref.shape[1]
    source = rows // 8
    width = weights_ref.shape[1]
    part = width // FOLD
    acc_main[...] = jnp.zeros_like(acc_main)
    acc_extra[...] = jnp.zeros_like(acc_extra)

    def step(m, carry):
        cols = columns(m, part)
        weights = weights_ref[:, cols]
        acc_main[...] += dot(weights, payload_ref[:, cols], 1, 1)
        acc_extra[...] += dot(weights, unfolded(payload_ref[:, width:], m), 1, 1)
        return carry

    lax.fori_loop(0, FOLD, step, 0)
    main, extra = acc_main[...], acc_extra[...]
    main_ref[...] = main.astype(BF16)
    extra_ref[...] = extra.astype(BF16)
    span = slice(half * units, (half + 1) * units)
    main_score = jnp.sum(main * main_t_ref[span, :].astype(F32), axis=0, keepdims=True)
    extra_score = jnp.sum(extra * extra_t_ref[span, :].astype(F32), axis=0, keepdims=True)
    to_main = iota((source, rows), 0) == iota((source, rows), 1) // 8
    at_main = iota((rows, 128), 0) % 8 == iota((rows, 128), 1)
    to_extra = iota((source, few), 0) == iota((source, few), 1) % source
    at_extra = iota((few, 128), 0) // source + 8 == iota((few, 128), 1)
    score = exact_dot(jnp.where(to_main, main_score, 0.0), jnp.where(at_main, 1.0, 0.0))
    score = score + exact_dot(jnp.where(to_extra, extra_score, 0.0), jnp.where(at_extra, 1.0, 0.0))
    if given:
        score = score + given[0][...]
    score_ref[...] = score


def half_product(main_t, extra_t, weights, payload, half, *given):
    units, rows = main_t.shape
    few = extra_t.shape[1]
    return pl.pallas_call(
        functools.partial(product_kernel, half),
        in_specs=[VMEM] * (4 + len(given)),
        out_specs=[VMEM] * 3,
        out_shape=[
            jax.ShapeDtypeStruct((units // 2, rows), BF16),
            jax.ShapeDtypeStruct((units // 2, few), BF16),
            jax.ShapeDtypeStruct((rows // 8, 128), F32),
        ],
        scratch_shapes=[pltpu.VMEM((units // 2, rows), F32), pltpu.VMEM((units // 2, few), F32)],
        compiler_params=PARAMS,
        cost_estimate=cost(units * (rows + few) * weights.shape[1], 0),
        name="product_of_other" if half else "product_of_own",
    )(main_t, extra_t, weights, payload, *given)


def order_kernel(shard, place_ref, own_main, own_extra, other_main, other_extra, grad_ref):
    half, rows = own_main.shape
    few = own_extra.shape[1]
    units = 2 * half
    source = rows // 8
    to_unit = permuted_units(place_ref[0], units, shard)
    column = onehot(iota((units, units), 0) == to_unit)
    here = iota((rows, rows), 0)
    turn = onehot(iota((rows, rows), 1) == (here % source) * 8 + here // source)
    keep = onehot(iota((few, few), 0) == iota((few, few), 1))
    own, other = column[:, :half], column[:, half:]
    main = (dot(own, own_main[...]) + dot(other, other_main[...])).astype(BF16)
    extra = (dot(own, own_extra[...]) + dot(other, other_extra[...])).astype(BF16)
    grad_ref[:rows, :] = dot(turn, main, 1, 1).astype(BF16)
    grad_ref[rows:, :] = dot(keep, extra, 1, 1).astype(BF16)


def exact_dot(a, b, ca=1, cb=0):
    return lax.dot_general(
        a,
        b,
        (((ca,), (cb,)), ((), ())),
        precision=lax.Precision.HIGHEST,
        preferred_element_type=F32,
    )


def placed_kernel(place_ref, *refs):
    *pieces, out_ref, sems = refs
    count = len(pieces)
    copies = []
    for k, piece in enumerate(pieces):
        base = lax.rem(place_ref[1] + k, count) * 2
        for t in range(2):
            spot = base + (place_ref[2] ^ t)
            copies.append(pltpu.make_async_copy(piece.at[t], out_ref.at[spot], sems.at[2 * k + t]))
            copies[-1].start()
    for copy in copies:
        copy.wait()


def gathered(place, pair):
    size = lax.axis_size("y")
    down = [(i, (i + size - 1) % size) for i in range(size)]
    up = [(i, (i + 1) % size) for i in range(size)]
    above = below = pair = in_hbm(pair)
    pieces = [pair] + [None] * (size - 1)
    for k in range(1, size // 2 + 1):
        above = in_hbm(lax.ppermute(above, "y", down))
        pieces[k] = above
        if k < size - k:
            below = in_hbm(lax.ppermute(below, "y", up))
            pieces[size - k] = below
    placed = pl.pallas_call(
        placed_kernel,
        in_specs=[SMEM] + [HBM] * size,
        out_specs=VMEM,
        out_shape=jax.ShapeDtypeStruct((2 * size, *pair.shape[1:]), pair.dtype),
        scratch_shapes=[pltpu.SemaphoreType.DMA((2 * size,))],
        compiler_params=PARAMS,
        cost_estimate=cost(0, 0),
        name="placed",
    )(place, *pieces)
    return placed


def pair_kernel(weights_ref, beside_ref, first_ref, out_ref):
    out_ref[0] = weights_ref[...]
    out_ref[1] = beside_ref[...]


def paired(weights, beside, first):
    return pl.pallas_call(
        pair_kernel,
        in_specs=[VMEM, VMEM, HBM],
        out_specs=VMEM,
        out_shape=jax.ShapeDtypeStruct((2, *weights.shape), weights.dtype),
        compiler_params=PARAMS,
        cost_estimate=cost(0, 0),
        name="paired",
    )(weights, beside, in_hbm(first))


def returned_scores(blocks):
    outer, inner = (lax.axis_size(k) for k in EXPERT)
    lanes = blocks.shape[1]
    row = lax.all_gather(blocks, "x").reshape(inner, outer, inner, lanes)
    row = lax.dynamic_index_in_dim(row, lax.axis_index("x"), 2, keepdims=False)
    square = lax.all_gather(row, "zh")
    square = lax.dynamic_index_in_dim(square, lax.axis_index("zh"), 2, keepdims=False)
    return square.reshape(outer * inner, lanes)


def in_hbm(array):
    return pltpu.with_memory_space_constraint(array, pltpu.HBM)


def after(array, first):
    return pl.pallas_call(
        after_kernel,
        in_specs=[HBM, VMEM],
        out_specs=HBM,
        out_shape=pltpu.HBM(array.shape, array.dtype),
        input_output_aliases={0: 0},
        cost_estimate=cost(0, 0),
        name="after",
    )(array, first)


def after_kernel(array_ref, first_ref, out_ref):
    pass


def sum_kernel(pieces_ref, out_ref):
    total = pieces_ref[0].astype(F32)
    for k in range(1, pieces_ref.shape[0]):
        total = total + pieces_ref[k].astype(F32)
    out_ref[...] = total


def summed(pieces):
    count, shard, width = pieces.shape
    part = width // 4
    return pl.pallas_call(
        sum_kernel,
        grid=(4,),
        in_specs=[pl.BlockSpec((count, shard, part), lambda g: (0, 0, g))],
        out_specs=pl.BlockSpec((shard, part), lambda g: (0, g)),
        out_shape=jax.ShapeDtypeStruct((shard, width), F32),
        compiler_params=PARAMS,
        cost_estimate=cost(count * shard * width, 2 * count * shard * width),
        name="summed",
    )(pieces)


def logits_kernel(logits_ref, chosen_ref, slots_ref, outside_ref, score_ref, out_ref):
    gating = softmax_rows(logits_ref[...])
    sent = gating.astype(BF16).astype(F32)
    chosen, slots = chosen_ref[...], slots_ref[...]
    topk, tokens = chosen.shape
    experts = score_ref.shape[0]
    returned = score_ref[...]
    found = []
    for k in range(topk):
        hit = jnp.where(iota((experts, tokens), 0) == chosen[k : k + 1, :], 1.0, 0.0)
        by_slot = exact_dot(returned, hit, 0, 0)[:16, :]
        at_slot = iota((16, tokens), 0) == slots[k : k + 1, :]
        found.append(jnp.sum(jnp.where(at_slot, by_slot, 0.0), axis=0, keepdims=True))
    inside = jnp.concatenate(found, axis=0) / sent
    outside = jnp.where(chosen >= experts, outside_ref[...], 0.0)
    scores = jnp.where(slots < 10, inside, outside)
    mean = jnp.sum(gating * scores, axis=0, keepdims=True)
    out_ref[...] = gating * (scores - mean)


def body(grad_output, logits, chosen, slots, other_scores, hidden, down_weight):
    tokens, topk = logits.shape
    window, capacity, units = hidden.shape[2], hidden.shape[3], hidden.shape[4]
    model = grad_output.shape[1]
    shard = down_weight.shape[1]
    place = jnp.stack([lax.axis_index(k) for k in ("core", "y", "zl")]).astype(jnp.int32)
    logits_t, chosen_t, slots_t = logits.T, chosen.T, slots.T
    swap = [(0, 1), (1, 0)]

    weights = down_weight.reshape(shard, model)
    beside = lax.ppermute(weights, "zl", swap)
    tile = jax.ShapeDtypeStruct((window * 8, tokens), BF16)
    placing = pl.pallas_call(
        place_kernel,
        in_specs=[HBM] * 3,
        out_specs=[VMEM] * 2,
        out_shape=[tile, tile],
        scratch_shapes=[
            pltpu.VMEM((topk, tokens), F32),
            pltpu.VMEM((topk, tokens), jnp.int32),
            pltpu.VMEM((topk, tokens), jnp.int32),
            pltpu.SemaphoreType.DMA((3,)),
        ],
        compiler_params=PARAMS,
        cost_estimate=cost(0, 4 * 320 * model),
        name="placing",
    )(*map(in_hbm, (logits_t, chosen_t, slots_t)))
    packed_shape = (window * 8, model + model // FOLD)
    packed = pl.pallas_call(
        pack_kernel,
        in_specs=[VMEM, VMEM, HBM],
        out_specs=HBM,
        out_shape=pltpu.HBM(packed_shape, BF16),
        scratch_shapes=[
            pltpu.VMEM((tokens, model), BF16),
            pltpu.VMEM(packed_shape, BF16),
            pltpu.SemaphoreType.DMA((FOLD + 2,)),
        ],
        compiler_params=PARAMS,
        cost_estimate=cost(2 * 320 * tokens * model * 2, 4 * 320 * model),
        name="pack",
    )(*placing, in_hbm(grad_output))
    packed = after(packed, beside[:8, :128])
    payload = lax.all_to_all(
        packed.reshape(window, 8, packed.shape[1]), EXPERT, split_axis=0, concat_axis=0, tiled=True
    ).reshape(packed.shape)

    own_weights = gathered(place, paired(weights, beside, packed))
    own_weights = own_weights.reshape(-1, model)
    other_weights = lax.ppermute(own_weights, "core", swap)

    by_slot = hidden.transpose(0, 1, 3, 2, 4).reshape(capacity * window, units)
    main_t, extra_t = pl.pallas_call(
        functools.partial(hidden_kernel, shard),
        in_specs=[SMEM, VMEM],
        out_specs=[VMEM] * 2,
        out_shape=[
            jax.ShapeDtypeStruct((units, window * 8), BF16),
            jax.ShapeDtypeStruct((units, window * 2), BF16),
        ],
        compiler_params=PARAMS,
        cost_estimate=cost(4 * 320 * units * units, 8 * 320 * units),
        name="hidden_order",
    )(place, by_slot)

    sent = half_partial(main_t, extra_t, payload, 1, first=(own_weights[:8, :128],))
    arrived = lax.ppermute(sent, "core", swap)
    both = half_partial(main_t, extra_t, payload, 0, arrived)
    parts = lax.all_to_all(
        both.reshape(-1, shard, model), RING, split_axis=0, concat_axis=0, tiled=True
    )
    grad_down = summed(parts).reshape(1, shard, model)

    *own_grad, score = half_product(main_t, extra_t, own_weights, payload, 0)
    *other_grad, score = half_product(main_t, extra_t, other_weights, payload, 1, score)
    returned = returned_scores(score)
    grad = pl.pallas_call(
        functools.partial(order_kernel, shard),
        in_specs=[SMEM] + [VMEM] * 4,
        out_specs=VMEM,
        out_shape=jax.ShapeDtypeStruct((capacity * window, units), BF16),
        compiler_params=PARAMS,
        cost_estimate=cost(2 * 320 * units * units, 4 * 320 * units),
        name="order",
    )(place, *own_grad, *other_grad)
    grad_hidden = grad.reshape(1, 1, capacity, window, units).transpose(0, 1, 3, 2, 4)
    grad_logits = pl.pallas_call(
        logits_kernel,
        in_specs=[VMEM] * 5,
        out_specs=VMEM,
        out_shape=jax.ShapeDtypeStruct((topk, tokens), F32),
        compiler_params=PARAMS,
        cost_estimate=cost(0, 0),
        name="logits",
    )(logits_t, chosen_t, slots_t, other_scores.T, returned)
    return grad_hidden, grad_down, grad_logits.T


def solution(mesh):
    torus = Mesh(mesh.devices.reshape(4, 8, 8, 2, 2), ALL)
    in_specs = (
        P(ALL, None),
        P(ALL, None),
        P(ALL, None),
        P(ALL, None),
        P(ALL, None),
        P(EXPERT, DP, None, None, None),
        P(EXPERT, DP, None),
    )
    out_specs = (P(EXPERT, DP, None, None, None), P(EXPERT, DP, None), P(ALL, None))
    return jax.shard_map(body, mesh=torus, in_specs=in_specs, out_specs=out_specs, check_vma=False)
```

```python
import functools

import jax
import jax.numpy as jnp
from jax import lax
from jax.experimental import pallas as pl
from jax.experimental.pallas import tpu as pltpu
from jax.sharding import Mesh
from jax.sharding import PartitionSpec as P

EXPERT = ("zh", "x")
RING = ("y", "zl")
DP = ("y", "zl", "core")
ALL = EXPERT + DP
FOLD = 4
F32 = jnp.float32
BF16 = jnp.bfloat16
VMEM = pl.BlockSpec(memory_space=pltpu.VMEM)
HBM = pl.BlockSpec(memory_space=pltpu.HBM)
SMEM = pl.BlockSpec(memory_space=pltpu.SMEM)
PARAMS = pltpu.CompilerParams(vmem_limit_bytes=12 * 1024 * 1024)


def cost(flops, size):
    return pl.CostEstimate(flops=flops, bytes_accessed=size, transcendentals=0)


def iota(shape, dim):
    return lax.broadcasted_iota(jnp.int32, shape, dim)


def onehot(mask):
    return jnp.where(mask, 1.0, 0.0).astype(BF16)


def dot(a, b, ca=1, cb=0):
    return lax.dot_general(a, b, (((ca,), (cb,)), ((), ())), preferred_element_type=F32)


def softmax_rows(logits):
    raised = jnp.exp(logits)
    return raised / jnp.sum(raised, axis=0, keepdims=True)


def place_kernel(logits_in, chosen_in, slots_in, place_ref, fold_ref, *scratch):
    held, sems = scratch[:3], scratch[3]
    copies = [
        pltpu.make_async_copy(src, dst, sems.at[k])
        for k, (src, dst) in enumerate(zip((logits_in, chosen_in, slots_in), held))
    ]
    for copy in copies:
        copy.start()
    for copy in copies:
        copy.wait()
    logits_ref, chosen_ref, slots_ref = held
    gate = softmax_rows(logits_ref[...]).astype(BF16).astype(F32)
    chosen, slots = chosen_ref[...], slots_ref[...]
    topk, tokens = chosen.shape
    rows = place_ref.shape[0]
    main = jnp.where(slots < 8, chosen * 8 + slots, -1)
    extra = jnp.where((slots >= 8) & (slots < 10), chosen * 2 + slots - 8, -1)
    row = iota((rows, tokens), 0)
    place = jnp.zeros((rows, tokens), F32)
    fold = jnp.zeros((rows, tokens), F32)
    for k in range(topk):
        place = jnp.where(row == main[k : k + 1, :], gate[k : k + 1, :], place)
        fold = jnp.where(row // FOLD == extra[k : k + 1, :], gate[k : k + 1, :], fold)
    place_ref[...] = place.astype(BF16)
    fold_ref[...] = fold.astype(BF16)


def pack_kernel(place_ref, fold_ref, rows_in, out_ref, rows_ref, held, sems):
    copy = pltpu.make_async_copy(rows_in, rows_ref, sems.at[0])
    copy.start()
    place, fold = place_ref[...], fold_ref[...].astype(F32)
    rows, tokens = place.shape
    row = iota((rows, tokens), 0)
    folds = [jnp.where(row % FOLD == m, fold, 0.0).astype(BF16) for m in range(FOLD)]
    part = rows_ref.shape[1] // FOLD
    total = jnp.zeros((rows, part), F32)
    copy.wait()
    copies = []
    for m in range(FOLD + 1):
        cols = slice(m * part, (m + 1) * part)
        if m < FOLD:
            block = rows_ref[:, cols]
            held[:, cols] = dot(place, block).astype(BF16)
            total = total + dot(folds[m], block)
        else:
            held[:, cols] = total.astype(BF16)
        copies.append(pltpu.make_async_copy(held.at[:, cols], out_ref.at[:, cols], sems.at[m + 1]))
        copies[-1].start()
    for copy in copies:
        copy.wait()


def permuted_units(core, units, shard):
    half = units // 2
    place = iota((1, units), 1)
    other = (place >= half).astype(jnp.int32)
    inner = place - other * half
    side = jnp.where(other == 1, 1 - core, core)
    block = inner // shard
    return block * (2 * shard) + side * shard + (inner - block * shard)


def hidden_kernel(shard, place_ref, hidden_ref, main_t_ref, extra_t_ref):
    units, rows = main_t_ref.shape
    to_unit = permuted_units(place_ref[0], units, shard)
    column = onehot(iota((units, units), 0) == to_unit)
    source = rows // 8
    here = iota((rows, rows), 0)
    there = iota((rows, rows), 1)
    turn = onehot(there == (here % 8) * source + here // 8)
    turned = dot(turn, hidden_ref[:rows, :]).astype(BF16)
    main_t_ref[...] = dot(column, turned, 0, 1).astype(BF16)
    extra_t_ref[...] = dot(column, hidden_ref[rows:, :], 0, 1).astype(BF16)


def unfolded(block, m):
    rows = block.shape[0]
    few = rows // FOLD
    source = rows // 8
    here = iota((few, rows), 0)
    there = iota((few, rows), 1)
    pick = onehot(there == (here % source) * 8 + (here // source) * FOLD + m)
    return dot(pick, block).astype(BF16)


def columns(m, part):
    return pl.ds(pl.multiple_of(m * part, part), part)


def half_kernel(half, adds, main_t_ref, extra_t_ref, payload_ref, *refs):
    *given, out_ref, held, sems = refs
    units, width = held.shape
    part = width // FOLD
    span = slice(half * units, (half + 1) * units)
    main_t, extra_t = main_t_ref[span, :], extra_t_ref[span, :]
    fold = payload_ref[:, width:]
    copies = []
    for m in range(FOLD):
        cols = slice(m * part, (m + 1) * part)
        total = dot(main_t, payload_ref[:, cols]) + dot(extra_t, unfolded(fold, m))
        if adds:
            total = total + given[0][:, cols].astype(F32)
        held[:, cols] = total.astype(BF16)
        copies.append(pltpu.make_async_copy(held.at[:, cols], out_ref.at[:, cols], sems.at[m]))
        copies[-1].start()
    for copy in copies:
        copy.wait()


def half_partial(main_t, extra_t, payload, half, arrived=None, first=()):
    given = [] if arrived is None else [arrived]
    units, rows = main_t.shape
    few = extra_t.shape[1]
    width = payload.shape[1] * FOLD // (FOLD + 1)
    return pl.pallas_call(
        functools.partial(half_kernel, half, bool(given)),
        in_specs=[VMEM] * (3 + len(given)) + [VMEM] * len(first),
        out_specs=HBM,
        out_shape=pltpu.HBM((units // 2, width), BF16),
        scratch_shapes=[pltpu.VMEM((units // 2, width), BF16), pltpu.SemaphoreType.DMA((FOLD,))],
        compiler_params=PARAMS,
        cost_estimate=cost(units * (rows + few) * width, 3 * units * width),
        name="half_kept" if given else "half_sent",
    )(main_t, extra_t, payload, *given, *first)


def product_kernel(half, place_ref, main_t_ref, extra_t_ref, weights_ref, payload_ref, *refs):
    *given, main_ref, extra_ref, score_ref, acc_main, acc_extra = refs
    units, rows = main_ref.shape
    few = extra_ref.shape[1]
    source = rows // 8
    width = weights_ref.shape[1]
    part = width // FOLD
    acc_main[...] = jnp.zeros_like(acc_main)
    acc_extra[...] = jnp.zeros_like(acc_extra)

    def step(m, carry):
        cols = columns(m, part)
        weights = weights_ref[:, cols]
        acc_main[...] += dot(weights, payload_ref[:, cols], 1, 1)
        acc_extra[...] += dot(weights, unfolded(payload_ref[:, width:], m), 1, 1)
        return carry

    lax.fori_loop(0, FOLD, step, 0)
    main, extra = acc_main[...], acc_extra[...]
    main_ref[...] = main.astype(BF16)
    extra_ref[...] = extra.astype(BF16)
    span = slice(half * units, (half + 1) * units)
    main_score = jnp.sum(main * main_t_ref[span, :].astype(F32), axis=0, keepdims=True)
    extra_score = jnp.sum(extra * extra_t_ref[span, :].astype(F32), axis=0, keepdims=True)
    to_main = (iota((source, rows), 0) ^ place_ref[3]) == iota((source, rows), 1) // 8
    at_main = iota((rows, 128), 0) % 8 == iota((rows, 128), 1)
    to_extra = (iota((source, few), 0) ^ place_ref[3]) == iota((source, few), 1) % source
    at_extra = iota((few, 128), 0) // source + 8 == iota((few, 128), 1)
    score = exact_dot(jnp.where(to_main, main_score, 0.0), jnp.where(at_main, 1.0, 0.0))
    score = score + exact_dot(jnp.where(to_extra, extra_score, 0.0), jnp.where(at_extra, 1.0, 0.0))
    if given:
        score = score + given[0][...]
    score_ref[...] = score


def half_product(place, main_t, extra_t, weights, payload, half, *given):
    units, rows = main_t.shape
    few = extra_t.shape[1]
    return pl.pallas_call(
        functools.partial(product_kernel, half),
        in_specs=[SMEM] + [VMEM] * (4 + len(given)),
        out_specs=[VMEM] * 3,
        out_shape=[
            jax.ShapeDtypeStruct((units // 2, rows), BF16),
            jax.ShapeDtypeStruct((units // 2, few), BF16),
            jax.ShapeDtypeStruct((rows // 8, 128), F32),
        ],
        scratch_shapes=[pltpu.VMEM((units // 2, rows), F32), pltpu.VMEM((units // 2, few), F32)],
        compiler_params=PARAMS,
        cost_estimate=cost(units * (rows + few) * weights.shape[1], 0),
        name="product_of_other" if half else "product_of_own",
    )(place, main_t, extra_t, weights, payload, *given)


def order_kernel(shard, place_ref, own_main, own_extra, other_main, other_extra, grad_ref):
    half, rows = own_main.shape
    few = own_extra.shape[1]
    units = 2 * half
    source = rows // 8
    to_unit = permuted_units(place_ref[0], units, shard)
    column = onehot(iota((units, units), 0) == to_unit)
    here = iota((rows, rows), 0)
    turn = onehot(iota((rows, rows), 1) == (here % source) * 8 + here // source)
    keep = onehot(iota((few, few), 0) == iota((few, few), 1))
    own, other = column[:, :half], column[:, half:]
    main = (dot(own, own_main[...]) + dot(other, other_main[...])).astype(BF16)
    extra = (dot(own, own_extra[...]) + dot(other, other_extra[...])).astype(BF16)
    grad_ref[:rows, :] = dot(turn, main, 1, 1).astype(BF16)
    grad_ref[rows:, :] = dot(keep, extra, 1, 1).astype(BF16)


def exact_dot(a, b, ca=1, cb=0):
    return lax.dot_general(
        a,
        b,
        (((ca,), (cb,)), ((), ())),
        precision=lax.Precision.HIGHEST,
        preferred_element_type=F32,
    )


def placed_kernel(place_ref, *refs):
    *pieces, out_ref, sems = refs
    count = len(pieces)
    copies = []
    for k, piece in enumerate(pieces):
        base = lax.rem(place_ref[1] + k, count) * 2
        for t in range(2):
            spot = base + (place_ref[2] ^ t)
            copies.append(pltpu.make_async_copy(piece.at[t], out_ref.at[spot], sems.at[2 * k + t]))
            copies[-1].start()
    for copy in copies:
        copy.wait()


def gathered(place, pair):
    size = lax.axis_size("y")
    down = [(i, (i + size - 1) % size) for i in range(size)]
    up = [(i, (i + 1) % size) for i in range(size)]
    above = below = pair = in_hbm(pair)
    pieces = [pair] + [None] * (size - 1)
    for k in range(1, size // 2 + 1):
        above = in_hbm(lax.ppermute(above, "y", down))
        pieces[k] = above
        if k < size - k:
            below = in_hbm(lax.ppermute(below, "y", up))
            pieces[size - k] = below
    placed = pl.pallas_call(
        placed_kernel,
        in_specs=[SMEM] + [HBM] * size,
        out_specs=VMEM,
        out_shape=jax.ShapeDtypeStruct((2 * size, *pair.shape[1:]), pair.dtype),
        scratch_shapes=[pltpu.SemaphoreType.DMA((2 * size,))],
        compiler_params=PARAMS,
        cost_estimate=cost(0, 0),
        name="placed",
    )(place, *pieces)
    return placed


def pair_kernel(weights_ref, beside_ref, first_ref, out_ref):
    out_ref[0] = weights_ref[...]
    out_ref[1] = beside_ref[...]


def paired(weights, beside, first):
    return pl.pallas_call(
        pair_kernel,
        in_specs=[VMEM, VMEM, HBM],
        out_specs=VMEM,
        out_shape=jax.ShapeDtypeStruct((2, *weights.shape), weights.dtype),
        compiler_params=PARAMS,
        cost_estimate=cost(0, 0),
        name="paired",
    )(weights, beside, in_hbm(first))


def exchanged_by_bits(blocks):
    count, lanes = blocks.shape
    inner = lax.axis_size("x")
    bit = 1
    while bit < count:
        axis, step = ("x", bit) if bit < inner else ("zh", bit // inner)
        size = lax.axis_size(axis)
        pairs = blocks.reshape(count // (2 * bit), 2, bit, lanes)
        came = lax.ppermute(pairs[:, 1], axis, [(i, i ^ step) for i in range(size)])
        blocks = jnp.stack([pairs[:, 0], came], axis=1).reshape(count, lanes)
        bit *= 2
    return blocks


def in_vmem(array):
    return pltpu.with_memory_space_constraint(array, pltpu.VMEM)


def in_hbm(array):
    return pltpu.with_memory_space_constraint(array, pltpu.HBM)


def after(array, first):
    return pl.pallas_call(
        after_kernel,
        in_specs=[HBM, VMEM],
        out_specs=HBM,
        out_shape=pltpu.HBM(array.shape, array.dtype),
        input_output_aliases={0: 0},
        cost_estimate=cost(0, 0),
        name="after",
    )(array, first)


def after_kernel(array_ref, first_ref, out_ref):
    pass


def sum_kernel(pieces_ref, out_ref):
    total = pieces_ref[0].astype(F32)
    for k in range(1, pieces_ref.shape[0]):
        total = total + pieces_ref[k].astype(F32)
    out_ref[...] = total


def summed(pieces):
    count, shard, width = pieces.shape
    part = width // 4
    return pl.pallas_call(
        sum_kernel,
        grid=(4,),
        in_specs=[pl.BlockSpec((count, shard, part), lambda g: (0, 0, g))],
        out_specs=pl.BlockSpec((shard, part), lambda g: (0, g)),
        out_shape=jax.ShapeDtypeStruct((shard, width), F32),
        compiler_params=PARAMS,
        cost_estimate=cost(count * shard * width, 2 * count * shard * width),
        name="summed",
    )(pieces)


def logits_kernel(place_ref, logits_ref, chosen_ref, slots_ref, outside_ref, score_ref, out_ref):
    gating = softmax_rows(logits_ref[...])
    sent = gating.astype(BF16).astype(F32)
    chosen, slots = chosen_ref[...], slots_ref[...]
    topk, tokens = chosen.shape
    experts = score_ref.shape[0]
    returned = score_ref[...]
    found = []
    here = chosen ^ place_ref[3]
    for k in range(topk):
        hit = jnp.where(iota((experts, tokens), 0) == here[k : k + 1, :], 1.0, 0.0)
        by_slot = exact_dot(returned, hit, 0, 0)[:16, :]
        at_slot = iota((16, tokens), 0) == slots[k : k + 1, :]
        found.append(jnp.sum(jnp.where(at_slot, by_slot, 0.0), axis=0, keepdims=True))
    inside = jnp.concatenate(found, axis=0) / sent
    outside = jnp.where(chosen >= experts, outside_ref[...], 0.0)
    scores = jnp.where(slots < 10, inside, outside)
    mean = jnp.sum(gating * scores, axis=0, keepdims=True)
    out_ref[...] = gating * (scores - mean)


def body(grad_output, logits, chosen, slots, other_scores, hidden, down_weight):
    tokens, topk = logits.shape
    window, capacity, units = hidden.shape[2], hidden.shape[3], hidden.shape[4]
    model = grad_output.shape[1]
    shard = down_weight.shape[1]
    place = jnp.stack([lax.axis_index(k) for k in ("core", "y", "zl", EXPERT)]).astype(jnp.int32)
    logits_t, chosen_t, slots_t = logits.T, chosen.T, slots.T
    swap = [(0, 1), (1, 0)]

    weights = down_weight.reshape(shard, model)
    beside = lax.ppermute(weights, "zl", swap)
    tile = jax.ShapeDtypeStruct((window * 8, tokens), BF16)
    placing = pl.pallas_call(
        place_kernel,
        in_specs=[HBM] * 3,
        out_specs=[VMEM] * 2,
        out_shape=[tile, tile],
        scratch_shapes=[
            pltpu.VMEM((topk, tokens), F32),
            pltpu.VMEM((topk, tokens), jnp.int32),
            pltpu.VMEM((topk, tokens), jnp.int32),
            pltpu.SemaphoreType.DMA((3,)),
        ],
        compiler_params=PARAMS,
        cost_estimate=cost(0, 4 * 320 * model),
        name="placing",
    )(*map(in_hbm, (logits_t, chosen_t, slots_t)))
    packed_shape = (window * 8, model + model // FOLD)
    packed = pl.pallas_call(
        pack_kernel,
        in_specs=[VMEM, VMEM, HBM],
        out_specs=HBM,
        out_shape=pltpu.HBM(packed_shape, BF16),
        scratch_shapes=[
            pltpu.VMEM((tokens, model), BF16),
            pltpu.VMEM(packed_shape, BF16),
            pltpu.SemaphoreType.DMA((FOLD + 2,)),
        ],
        compiler_params=PARAMS,
        cost_estimate=cost(2 * 320 * tokens * model * 2, 4 * 320 * model),
        name="pack",
    )(*placing, in_hbm(grad_output))
    packed = after(packed, beside[:8, :128])
    payload = lax.all_to_all(
        packed.reshape(window, 8, packed.shape[1]), EXPERT, split_axis=0, concat_axis=0, tiled=True
    ).reshape(packed.shape)

    own_weights = gathered(place, paired(weights, beside, packed))
    own_weights = own_weights.reshape(-1, model)
    other_weights = in_vmem(lax.ppermute(own_weights, "core", swap))

    by_slot = hidden.transpose(0, 1, 3, 2, 4).reshape(capacity * window, units)
    main_t, extra_t = pl.pallas_call(
        functools.partial(hidden_kernel, shard),
        in_specs=[SMEM, VMEM],
        out_specs=[VMEM] * 2,
        out_shape=[
            jax.ShapeDtypeStruct((units, window * 8), BF16),
            jax.ShapeDtypeStruct((units, window * 2), BF16),
        ],
        compiler_params=PARAMS,
        cost_estimate=cost(4 * 320 * units * units, 8 * 320 * units),
        name="hidden_order",
    )(place, by_slot)

    sent = half_partial(main_t, extra_t, payload, 1, first=(own_weights[:8, :128],))
    arrived = lax.ppermute(sent, "core", swap)
    *own_grad, score = half_product(place, main_t, extra_t, own_weights, payload, 0)
    *other_grad, score = half_product(place, main_t, extra_t, other_weights, payload, 1, score)
    both = half_partial(main_t, extra_t, payload, 0, arrived, first=(score,))
    parts = lax.all_to_all(
        both.reshape(-1, shard, model), RING, split_axis=0, concat_axis=0, tiled=True
    )
    grad_down = summed(in_vmem(parts)).reshape(1, shard, model)

    returned = exchanged_by_bits(score)
    grad = pl.pallas_call(
        functools.partial(order_kernel, shard),
        in_specs=[SMEM] + [VMEM] * 4,
        out_specs=VMEM,
        out_shape=jax.ShapeDtypeStruct((capacity * window, units), BF16),
        compiler_params=PARAMS,
        cost_estimate=cost(2 * 320 * units * units, 4 * 320 * units),
        name="order",
    )(place, *own_grad, *other_grad)
    grad_hidden = grad.reshape(1, 1, capacity, window, units).transpose(0, 1, 3, 2, 4)
    grad_logits = pl.pallas_call(
        logits_kernel,
        in_specs=[SMEM] + [VMEM] * 5,
        out_specs=VMEM,
        out_shape=jax.ShapeDtypeStruct((topk, tokens), F32),
        compiler_params=PARAMS,
        cost_estimate=cost(0, 0),
        name="logits",
    )(place, logits_t, chosen_t, slots_t, other_scores.T, returned)
    return grad_hidden, grad_down, grad_logits.T


def solution(mesh):
    torus = Mesh(mesh.devices.reshape(4, 8, 8, 2, 2), ALL)
    in_specs = (
        P(ALL, None),
        P(ALL, None),
        P(ALL, None),
        P(ALL, None),
        P(ALL, None),
        P(EXPERT, DP, None, None, None),
        P(EXPERT, DP, None),
    )
    out_specs = (P(EXPERT, DP, None, None, None), P(EXPERT, DP, None), P(ALL, None))
    return jax.shard_map(body, mesh=torus, in_specs=in_specs, out_specs=out_specs, check_vma=False)
```

```python
import functools

import jax
import jax.numpy as jnp
from jax import lax
from jax.experimental import pallas as pl
from jax.experimental.pallas import tpu as pltpu
from jax.sharding import Mesh
from jax.sharding import PartitionSpec as P

EXPERT = ("zh", "x")
RING = ("y", "zl")
DP = ("y", "zl", "core")
ALL = EXPERT + DP
FOLD = 4
F32 = jnp.float32
BF16 = jnp.bfloat16
VMEM = pl.BlockSpec(memory_space=pltpu.VMEM)
HBM = pl.BlockSpec(memory_space=pltpu.HBM)
SMEM = pl.BlockSpec(memory_space=pltpu.SMEM)
PARAMS = pltpu.CompilerParams(vmem_limit_bytes=12 * 1024 * 1024)


def cost(flops, size):
    return pl.CostEstimate(flops=flops, bytes_accessed=size, transcendentals=0)


def iota(shape, dim):
    return lax.broadcasted_iota(jnp.int32, shape, dim)


def onehot(mask):
    return jnp.where(mask, 1.0, 0.0).astype(BF16)


def dot(a, b, ca=1, cb=0):
    return lax.dot_general(a, b, (((ca,), (cb,)), ((), ())), preferred_element_type=F32)


def softmax_rows(logits):
    raised = jnp.exp(logits)
    return raised / jnp.sum(raised, axis=0, keepdims=True)


def place_kernel(logits_in, chosen_in, slots_in, place_ref, fold_ref, *scratch):
    held, sems = scratch[:3], scratch[3]
    copies = [
        pltpu.make_async_copy(src, dst, sems.at[k])
        for k, (src, dst) in enumerate(zip((logits_in, chosen_in, slots_in), held))
    ]
    for copy in copies:
        copy.start()
    for copy in copies:
        copy.wait()
    logits_ref, chosen_ref, slots_ref = held
    gate = softmax_rows(logits_ref[...]).astype(BF16).astype(F32)
    chosen, slots = chosen_ref[...], slots_ref[...]
    topk, tokens = chosen.shape
    rows = place_ref.shape[0]
    main = jnp.where(slots < 8, chosen * 8 + slots, -1)
    extra = jnp.where((slots >= 8) & (slots < 10), chosen * 2 + slots - 8, -1)
    row = iota((rows, tokens), 0)
    place = jnp.zeros((rows, tokens), F32)
    fold = jnp.zeros((rows, tokens), F32)
    for k in range(topk):
        place = jnp.where(row == main[k : k + 1, :], gate[k : k + 1, :], place)
        fold = jnp.where(row // FOLD == extra[k : k + 1, :], gate[k : k + 1, :], fold)
    place_ref[...] = place.astype(BF16)
    fold_ref[...] = fold.astype(BF16)


def pack_kernel(place_ref, fold_ref, rows_in, out_ref, rows_ref, held, sems):
    copy = pltpu.make_async_copy(rows_in, rows_ref, sems.at[0])
    copy.start()
    place, fold = place_ref[...], fold_ref[...].astype(F32)
    rows, tokens = place.shape
    row = iota((rows, tokens), 0)
    folds = [jnp.where(row % FOLD == m, fold, 0.0).astype(BF16) for m in range(FOLD)]
    part = rows_ref.shape[1] // FOLD
    total = jnp.zeros((rows, part), F32)
    copy.wait()
    copies = []
    for m in range(FOLD + 1):
        cols = slice(m * part, (m + 1) * part)
        if m < FOLD:
            block = rows_ref[:, cols]
            held[:, cols] = dot(place, block).astype(BF16)
            total = total + dot(folds[m], block)
        else:
            held[:, cols] = total.astype(BF16)
        copies.append(pltpu.make_async_copy(held.at[:, cols], out_ref.at[:, cols], sems.at[m + 1]))
        copies[-1].start()
    for copy in copies:
        copy.wait()


def permuted_units(core, units, shard):
    half = units // 2
    place = iota((1, units), 1)
    other = (place >= half).astype(jnp.int32)
    inner = place - other * half
    side = jnp.where(other == 1, 1 - core, core)
    block = inner // shard
    return block * (2 * shard) + side * shard + (inner - block * shard)


def hidden_kernel(shard, place_ref, hidden_ref, main_t_ref, extra_t_ref):
    units, rows = main_t_ref.shape
    to_unit = permuted_units(place_ref[0], units, shard)
    column = onehot(iota((units, units), 0) == to_unit)
    source = rows // 8
    here = iota((rows, rows), 0)
    there = iota((rows, rows), 1)
    turn = onehot(there == (here % 8) * source + here // 8)
    turned = dot(turn, hidden_ref[:rows, :]).astype(BF16)
    main_t_ref[...] = dot(column, turned, 0, 1).astype(BF16)
    extra_t_ref[...] = dot(column, hidden_ref[rows:, :], 0, 1).astype(BF16)


def unfolded(block, m):
    rows = block.shape[0]
    few = rows // FOLD
    source = rows // 8
    here = iota((few, rows), 0)
    there = iota((few, rows), 1)
    pick = onehot(there == (here % source) * 8 + (here // source) * FOLD + m)
    return dot(pick, block).astype(BF16)


def columns(m, part):
    return pl.ds(pl.multiple_of(m * part, part), part)


def half_kernel(half, adds, main_t_ref, extra_t_ref, payload_ref, *refs):
    *given, out_ref, held, sems = refs
    units, width = held.shape
    part = width // FOLD
    span = slice(half * units, (half + 1) * units)
    main_t, extra_t = main_t_ref[span, :], extra_t_ref[span, :]
    fold = payload_ref[:, width:]
    copies = []
    for m in range(FOLD):
        cols = slice(m * part, (m + 1) * part)
        total = dot(main_t, payload_ref[:, cols]) + dot(extra_t, unfolded(fold, m))
        if adds:
            total = total + given[0][:, cols].astype(F32)
        held[:, cols] = total.astype(BF16)
        copies.append(pltpu.make_async_copy(held.at[:, cols], out_ref.at[:, cols], sems.at[m]))
        copies[-1].start()
    for copy in copies:
        copy.wait()


def half_partial(main_t, extra_t, payload, half, arrived=None, first=()):
    given = [] if arrived is None else [arrived]
    units, rows = main_t.shape
    few = extra_t.shape[1]
    width = payload.shape[1] * FOLD // (FOLD + 1)
    return pl.pallas_call(
        functools.partial(half_kernel, half, bool(given)),
        in_specs=[VMEM] * (3 + len(given)) + [VMEM] * len(first),
        out_specs=HBM,
        out_shape=pltpu.HBM((units // 2, width), BF16),
        scratch_shapes=[pltpu.VMEM((units // 2, width), BF16), pltpu.SemaphoreType.DMA((FOLD,))],
        compiler_params=PARAMS,
        cost_estimate=cost(units * (rows + few) * width, 3 * units * width),
        name="half_kept" if given else "half_sent",
    )(main_t, extra_t, payload, *given, *first)


def product_kernel(half, place_ref, main_t_ref, extra_t_ref, weights_ref, payload_ref, *refs):
    *given, main_ref, extra_ref, score_ref, acc_main, acc_extra = refs[: len(refs) - 2 * half]
    units, rows = main_ref.shape
    few = extra_ref.shape[1]
    source = rows // 8
    width = weights_ref.shape[1]
    part = width // FOLD
    acc_main[...] = jnp.zeros_like(acc_main)
    acc_extra[...] = jnp.zeros_like(acc_extra)
    source_ref = weights_ref
    if half:
        weights_ref, sems = refs[-2:]

    def copy_of(m):
        cols = columns(m, part)
        return pltpu.make_async_copy(source_ref.at[:, cols], weights_ref.at[:, cols], sems.at[m])

    def step(m, carry):
        cols = columns(m, part)
        if half:
            copy_of(m).wait()
        weights = weights_ref[:, cols]
        acc_main[...] += dot(weights, payload_ref[:, cols], 1, 1)
        acc_extra[...] += dot(weights, unfolded(payload_ref[:, width:], m), 1, 1)
        return carry

    if half:
        for m in range(FOLD):
            copy_of(m).start()
    lax.fori_loop(0, FOLD, step, 0)
    main, extra = acc_main[...], acc_extra[...]
    main_ref[...] = main.astype(BF16)
    extra_ref[...] = extra.astype(BF16)
    span = slice(half * units, (half + 1) * units)
    main_score = jnp.sum(main * main_t_ref[span, :].astype(F32), axis=0, keepdims=True)
    extra_score = jnp.sum(extra * extra_t_ref[span, :].astype(F32), axis=0, keepdims=True)
    to_main = (iota((source, rows), 0) ^ place_ref[3]) == iota((source, rows), 1) // 8
    at_main = iota((rows, 128), 0) % 8 == iota((rows, 128), 1)
    to_extra = (iota((source, few), 0) ^ place_ref[3]) == iota((source, few), 1) % source
    at_extra = iota((few, 128), 0) // source + 8 == iota((few, 128), 1)
    score = exact_dot(jnp.where(to_main, main_score, 0.0), jnp.where(at_main, 1.0, 0.0))
    score = score + exact_dot(jnp.where(to_extra, extra_score, 0.0), jnp.where(at_extra, 1.0, 0.0))
    if given:
        score = score + given[0][...]
    score_ref[...] = score


def half_product(place, main_t, extra_t, weights, payload, half, *given):
    units, rows = main_t.shape
    few = extra_t.shape[1]
    return pl.pallas_call(
        functools.partial(product_kernel, half),
        in_specs=[SMEM, VMEM, VMEM, HBM if half else VMEM, VMEM] + [VMEM] * len(given),
        out_specs=[VMEM] * 3,
        out_shape=[
            jax.ShapeDtypeStruct((units // 2, rows), BF16),
            jax.ShapeDtypeStruct((units // 2, few), BF16),
            jax.ShapeDtypeStruct((rows // 8, 128), F32),
        ],
        scratch_shapes=[pltpu.VMEM((units // 2, rows), F32), pltpu.VMEM((units // 2, few), F32)]
        + [pltpu.VMEM(weights.shape, BF16), pltpu.SemaphoreType.DMA((FOLD,))][: 2 * half],
        compiler_params=PARAMS,
        cost_estimate=cost(units * (rows + few) * weights.shape[1], 0),
        name="product_of_other" if half else "product_of_own",
    )(place, main_t, extra_t, weights, payload, *given)


def order_kernel(shard, place_ref, own_main, own_extra, other_main, other_extra, grad_ref):
    half, rows = own_main.shape
    few = own_extra.shape[1]
    units = 2 * half
    source = rows // 8
    to_unit = permuted_units(place_ref[0], units, shard)
    column = onehot(iota((units, units), 0) == to_unit)
    here = iota((rows, rows), 0)
    turn = onehot(iota((rows, rows), 1) == (here % source) * 8 + here // source)
    keep = onehot(iota((few, few), 0) == iota((few, few), 1))
    own, other = column[:, :half], column[:, half:]
    main = (dot(own, own_main[...]) + dot(other, other_main[...])).astype(BF16)
    extra = (dot(own, own_extra[...]) + dot(other, other_extra[...])).astype(BF16)
    grad_ref[:rows, :] = dot(turn, main, 1, 1).astype(BF16)
    grad_ref[rows:, :] = dot(keep, extra, 1, 1).astype(BF16)


def exact_dot(a, b, ca=1, cb=0):
    return lax.dot_general(
        a,
        b,
        (((ca,), (cb,)), ((), ())),
        precision=lax.Precision.HIGHEST,
        preferred_element_type=F32,
    )


def placed_kernel(place_ref, *refs):
    *pieces, out_ref, sems = refs
    count = len(pieces)
    copies = []
    for k, piece in enumerate(pieces):
        base = lax.rem(place_ref[1] + (1 - 2 * place_ref[0]) * k + count, count) * 2
        for t in range(2):
            spot = base + (place_ref[2] ^ t)
            copies.append(pltpu.make_async_copy(piece.at[t], out_ref.at[spot], sems.at[2 * k + t]))
            copies[-1].start()
    for copy in copies:
        copy.wait()


def gathered(place, pair):
    size, cores = lax.axis_size("y"), lax.axis_size("core")

    def moves(step):
        return [
            (y * cores + core, (y + (step if core else -step)) % size * cores + core)
            for y in range(size)
            for core in range(cores)
        ]

    first = second = pair = in_hbm(pair)
    pieces = [pair] + [None] * (size - 1)
    for k in range(1, size // 2 + 1):
        first = in_hbm(lax.ppermute(first, ("y", "core"), moves(1)))
        pieces[k] = first
        if k < size - k:
            second = in_hbm(lax.ppermute(second, ("y", "core"), moves(-1)))
            pieces[size - k] = second
    placed = pl.pallas_call(
        placed_kernel,
        in_specs=[SMEM] + [HBM] * size,
        out_specs=VMEM,
        out_shape=jax.ShapeDtypeStruct((2 * size, *pair.shape[1:]), pair.dtype),
        scratch_shapes=[pltpu.SemaphoreType.DMA((2 * size,))],
        compiler_params=PARAMS,
        cost_estimate=cost(0, 0),
        name="placed",
    )(place, *pieces)
    return placed


def pair_kernel(weights_ref, beside_ref, first_ref, out_ref, sems):
    copies = [
        pltpu.make_async_copy(piece, out_ref.at[k], sems.at[k])
        for k, piece in enumerate((weights_ref, beside_ref))
    ]
    for copy in copies:
        copy.start()
    for copy in copies:
        copy.wait()


def paired(weights, beside, first):
    return pl.pallas_call(
        pair_kernel,
        in_specs=[HBM, HBM, HBM],
        out_specs=VMEM,
        out_shape=jax.ShapeDtypeStruct((2, *weights.shape), weights.dtype),
        scratch_shapes=[pltpu.SemaphoreType.DMA((2,))],
        compiler_params=PARAMS,
        cost_estimate=cost(0, 0),
        name="paired",
    )(in_hbm(weights), beside, in_hbm(first))


def exchanged_by_bits(blocks):
    count, lanes = blocks.shape
    inner = lax.axis_size("x")
    bit = 1
    while bit < count:
        axis, step = ("x", bit) if bit < inner else ("zh", bit // inner)
        size = lax.axis_size(axis)
        pairs = blocks.reshape(count // (2 * bit), 2, bit, lanes)
        came = lax.ppermute(pairs[:, 1], axis, [(i, i ^ step) for i in range(size)])
        blocks = jnp.stack([pairs[:, 0], came], axis=1).reshape(count, lanes)
        bit *= 2
    return blocks


def in_vmem(array):
    return pltpu.with_memory_space_constraint(array, pltpu.VMEM)


def in_hbm(array):
    return pltpu.with_memory_space_constraint(array, pltpu.HBM)


def after(array, first):
    return pl.pallas_call(
        after_kernel,
        in_specs=[HBM, HBM],
        out_specs=HBM,
        out_shape=pltpu.HBM(array.shape, array.dtype),
        input_output_aliases={0: 0},
        cost_estimate=cost(0, 0),
        name="after",
    )(array, first)


def after_kernel(array_ref, first_ref, out_ref):
    pass


def sum_kernel(pieces_ref, out_ref):
    total = pieces_ref[0].astype(F32)
    for k in range(1, pieces_ref.shape[0]):
        total = total + pieces_ref[k].astype(F32)
    out_ref[...] = total


def summed(pieces):
    count, shard, width = pieces.shape
    part = width // 4
    return pl.pallas_call(
        sum_kernel,
        grid=(4,),
        in_specs=[pl.BlockSpec((count, shard, part), lambda g: (0, 0, g))],
        out_specs=pl.BlockSpec((shard, part), lambda g: (0, g)),
        out_shape=pltpu.HBM((shard, width), F32),
        compiler_params=PARAMS,
        cost_estimate=cost(count * shard * width, 2 * count * shard * width),
        name="summed",
    )(pieces)


def logits_kernel(
    place_ref, logits_ref, chosen_ref, slots_ref, outside_ref, score_ref, first_ref, out_ref
):
    gating = softmax_rows(logits_ref[...])
    sent = gating.astype(BF16).astype(F32)
    chosen, slots = chosen_ref[...], slots_ref[...]
    topk, tokens = chosen.shape
    experts = score_ref.shape[0]
    returned = score_ref[:, :16]
    found = []
    here = chosen ^ place_ref[3]
    for k in range(topk):
        hit = jnp.where(iota((experts, tokens), 0) == here[k : k + 1, :], 1.0, 0.0)
        by_slot = exact_dot(returned, hit, 0, 0)
        at_slot = iota((16, tokens), 0) == slots[k : k + 1, :]
        found.append(jnp.sum(jnp.where(at_slot, by_slot, 0.0), axis=0, keepdims=True))
    inside = jnp.concatenate(found, axis=0) / sent
    outside = jnp.where(chosen >= experts, outside_ref[...], 0.0)
    scores = jnp.where(slots < 10, inside, outside)
    mean = jnp.sum(gating * scores, axis=0, keepdims=True)
    out_ref[...] = gating * (scores - mean)


def body(grad_output, logits, chosen, slots, other_scores, hidden, down_weight):
    tokens, topk = logits.shape
    window, capacity, units = hidden.shape[2], hidden.shape[3], hidden.shape[4]
    model = grad_output.shape[1]
    shard = down_weight.shape[1]
    place = jnp.stack([lax.axis_index(k) for k in ("core", "y", "zl", EXPERT)]).astype(jnp.int32)
    logits_t, chosen_t, slots_t = logits.T, chosen.T, slots.T
    swap = [(0, 1), (1, 0)]

    weights = down_weight.reshape(shard, model)
    beside = in_hbm(lax.ppermute(weights, "zl", swap))
    tile = jax.ShapeDtypeStruct((window * 8, tokens), BF16)
    placing = pl.pallas_call(
        place_kernel,
        in_specs=[HBM] * 3,
        out_specs=[VMEM] * 2,
        out_shape=[tile, tile],
        scratch_shapes=[
            pltpu.VMEM((topk, tokens), F32),
            pltpu.VMEM((topk, tokens), jnp.int32),
            pltpu.VMEM((topk, tokens), jnp.int32),
            pltpu.SemaphoreType.DMA((3,)),
        ],
        compiler_params=PARAMS,
        cost_estimate=cost(0, 4 * 320 * model),
        name="placing",
    )(*map(in_hbm, (logits_t, chosen_t, slots_t)))
    packed_shape = (window * 8, model + model // FOLD)
    packed = pl.pallas_call(
        pack_kernel,
        in_specs=[VMEM, VMEM, HBM],
        out_specs=HBM,
        out_shape=pltpu.HBM(packed_shape, BF16),
        scratch_shapes=[
            pltpu.VMEM((tokens, model), BF16),
            pltpu.VMEM(packed_shape, BF16),
            pltpu.SemaphoreType.DMA((FOLD + 2,)),
        ],
        compiler_params=PARAMS,
        cost_estimate=cost(2 * 320 * tokens * model * 2, 4 * 320 * model),
        name="pack",
    )(*placing, in_hbm(grad_output))
    packed = after(packed, beside)
    payload = lax.all_to_all(
        packed.reshape(window, 8, packed.shape[1]), EXPERT, split_axis=0, concat_axis=0, tiled=True
    ).reshape(packed.shape)

    own_weights = gathered(place, paired(weights, beside, packed))
    own_weights = own_weights.reshape(-1, model)
    other_weights = in_hbm(lax.ppermute(own_weights, "core", swap))

    by_slot = hidden.transpose(0, 1, 3, 2, 4).reshape(capacity * window, units)
    main_t, extra_t = pl.pallas_call(
        functools.partial(hidden_kernel, shard),
        in_specs=[SMEM, VMEM],
        out_specs=[VMEM] * 2,
        out_shape=[
            jax.ShapeDtypeStruct((units, window * 8), BF16),
            jax.ShapeDtypeStruct((units, window * 2), BF16),
        ],
        compiler_params=PARAMS,
        cost_estimate=cost(4 * 320 * units * units, 8 * 320 * units),
        name="hidden_order",
    )(place, by_slot)

    sent = half_partial(main_t, extra_t, payload, 1, first=(own_weights[:8, :128],))
    arrived = lax.ppermute(sent, "core", swap)
    *own_grad, score = half_product(place, main_t, extra_t, own_weights, payload, 0)
    *other_grad, score = half_product(place, main_t, extra_t, other_weights, payload, 1, score)
    both = half_partial(main_t, extra_t, payload, 0, arrived, first=(score,))
    parts = lax.all_to_all(
        both.reshape(-1, shard, model), RING, split_axis=0, concat_axis=0, tiled=True
    )
    total = summed(in_vmem(parts))
    grad_down = total.reshape(1, shard, model)

    returned = exchanged_by_bits(score)
    grad = pl.pallas_call(
        functools.partial(order_kernel, shard),
        in_specs=[SMEM] + [VMEM] * 4,
        out_specs=VMEM,
        out_shape=jax.ShapeDtypeStruct((capacity * window, units), BF16),
        compiler_params=PARAMS,
        cost_estimate=cost(2 * 320 * units * units, 4 * 320 * units),
        name="order",
    )(place, *own_grad, *other_grad)
    grad_hidden = grad.reshape(1, 1, capacity, window, units).transpose(0, 1, 3, 2, 4)
    grad_logits = pl.pallas_call(
        logits_kernel,
        in_specs=[SMEM] + [VMEM] * 5 + [HBM],
        out_specs=VMEM,
        out_shape=jax.ShapeDtypeStruct((topk, tokens), F32),
        compiler_params=PARAMS,
        cost_estimate=cost(0, 0),
        name="logits",
    )(place, logits_t, chosen_t, slots_t, other_scores.T, returned, in_hbm(total))
    return grad_hidden, grad_down, grad_logits.T


def solution(mesh):
    torus = Mesh(mesh.devices.reshape(4, 8, 8, 2, 2), ALL)
    in_specs = (
        P(ALL, None),
        P(ALL, None),
        P(ALL, None),
        P(ALL, None),
        P(ALL, None),
        P(EXPERT, DP, None, None, None),
        P(EXPERT, DP, None),
    )
    out_specs = (P(EXPERT, DP, None, None, None), P(EXPERT, DP, None), P(ALL, None))
    return jax.shard_map(body, mesh=torus, in_specs=in_specs, out_specs=out_specs, check_vma=False)
```

```python
import functools

import jax
import jax.numpy as jnp
from jax import lax
from jax.experimental import pallas as pl
from jax.experimental.pallas import tpu as pltpu
from jax.sharding import Mesh
from jax.sharding import PartitionSpec as P

EXPERT = ("zh", "x")
RING = ("y", "zl")
DP = ("y", "zl", "core")
ALL = EXPERT + DP
FOLD = 4
F32 = jnp.float32
BF16 = jnp.bfloat16
VMEM = pl.BlockSpec(memory_space=pltpu.VMEM)
HBM = pl.BlockSpec(memory_space=pltpu.HBM)
SMEM = pl.BlockSpec(memory_space=pltpu.SMEM)
PARAMS = pltpu.CompilerParams(vmem_limit_bytes=12 * 1024 * 1024)


def cost(flops, size):
    return pl.CostEstimate(flops=flops, bytes_accessed=size, transcendentals=0)


def iota(shape, dim):
    return lax.broadcasted_iota(jnp.int32, shape, dim)


def onehot(mask):
    return jnp.where(mask, 1.0, 0.0).astype(BF16)


def dot(a, b, ca=1, cb=0):
    return lax.dot_general(a, b, (((ca,), (cb,)), ((), ())), preferred_element_type=F32)


def softmax_rows(logits):
    raised = jnp.exp(logits)
    return raised / jnp.sum(raised, axis=0, keepdims=True)


def place_kernel(logits_in, chosen_in, slots_in, place_ref, fold_ref, *scratch):
    held, sems = scratch[:3], scratch[3]
    copies = [
        pltpu.make_async_copy(src, dst, sems.at[k])
        for k, (src, dst) in enumerate(zip((logits_in, chosen_in, slots_in), held))
    ]
    for copy in copies:
        copy.start()
    for copy in copies:
        copy.wait()
    logits_ref, chosen_ref, slots_ref = held
    gate = softmax_rows(logits_ref[...]).astype(BF16).astype(F32)
    chosen, slots = chosen_ref[...], slots_ref[...]
    topk, tokens = chosen.shape
    rows = place_ref.shape[0]
    main = jnp.where(slots < 8, chosen * 8 + slots, -1)
    extra = jnp.where((slots >= 8) & (slots < 10), chosen * 2 + slots - 8, -1)
    row = iota((rows, tokens), 0)
    place = jnp.zeros((rows, tokens), F32)
    fold = jnp.zeros((rows, tokens), F32)
    for k in range(topk):
        place = jnp.where(row == main[k : k + 1, :], gate[k : k + 1, :], place)
        fold = jnp.where(row // FOLD == extra[k : k + 1, :], gate[k : k + 1, :], fold)
    place_ref[...] = place.astype(BF16)
    fold_ref[...] = fold.astype(BF16)


def pack_kernel(place_ref, fold_ref, rows_in, out_ref, rows_ref, held, sems):
    copy = pltpu.make_async_copy(rows_in, rows_ref, sems.at[0])
    copy.start()
    place, fold = place_ref[...], fold_ref[...].astype(F32)
    rows, tokens = place.shape
    row = iota((rows, tokens), 0)
    folds = [jnp.where(row % FOLD == m, fold, 0.0).astype(BF16) for m in range(FOLD)]
    part = rows_ref.shape[1] // FOLD
    total = jnp.zeros((rows, part), F32)
    copy.wait()
    copies = []
    for m in range(FOLD + 1):
        cols = slice(m * part, (m + 1) * part)
        if m < FOLD:
            block = rows_ref[:, cols]
            held[:, cols] = dot(place, block).astype(BF16)
            total = total + dot(folds[m], block)
        else:
            held[:, cols] = total.astype(BF16)
        copies.append(pltpu.make_async_copy(held.at[:, cols], out_ref.at[:, cols], sems.at[m + 1]))
        copies[-1].start()
    for copy in copies:
        copy.wait()


def permuted_units(core, units, shard):
    half = units // 2
    place = iota((1, units), 1)
    other = (place >= half).astype(jnp.int32)
    inner = place - other * half
    side = jnp.where(other == 1, 1 - core, core)
    block = inner // shard
    return block * (2 * shard) + side * shard + (inner - block * shard)


def hidden_kernel(shard, place_ref, hidden_ref, main_t_ref, extra_t_ref):
    units, rows = main_t_ref.shape
    to_unit = permuted_units(place_ref[0], units, shard)
    column = onehot(iota((units, units), 0) == to_unit)
    source = rows // 8
    here = iota((rows, rows), 0)
    there = iota((rows, rows), 1)
    turn = onehot(there == (here % 8) * source + here // 8)
    turned = dot(turn, hidden_ref[:rows, :]).astype(BF16)
    main_t_ref[...] = dot(column, turned, 0, 1).astype(BF16)
    extra_t_ref[...] = dot(column, hidden_ref[rows:, :], 0, 1).astype(BF16)


def unfolded(block, m):
    rows = block.shape[0]
    few = rows // FOLD
    source = rows // 8
    here = iota((few, rows), 0)
    there = iota((few, rows), 1)
    pick = onehot(there == (here % source) * 8 + (here // source) * FOLD + m)
    return dot(pick, block).astype(BF16)


def columns(m, part):
    return pl.ds(pl.multiple_of(m * part, part), part)


def half_kernel(half, adds, main_t_ref, extra_t_ref, payload_ref, *refs):
    *given, out_ref, held, sems = refs
    units, width = held.shape
    part = width // FOLD
    span = slice(half * units, (half + 1) * units)
    main_t, extra_t = main_t_ref[span, :], extra_t_ref[span, :]
    fold = payload_ref[:, width:]
    copies = []
    for m in range(FOLD):
        cols = slice(m * part, (m + 1) * part)
        total = dot(main_t, payload_ref[:, cols]) + dot(extra_t, unfolded(fold, m))
        if adds:
            total = total + given[0][:, cols].astype(F32)
        held[:, cols] = total.astype(BF16)
        copies.append(pltpu.make_async_copy(held.at[:, cols], out_ref.at[:, cols], sems.at[m]))
        copies[-1].start()
    for copy in copies:
        copy.wait()


def half_partial(main_t, extra_t, payload, half, arrived=None, first=()):
    given = [] if arrived is None else [arrived]
    units, rows = main_t.shape
    few = extra_t.shape[1]
    width = payload.shape[1] * FOLD // (FOLD + 1)
    return pl.pallas_call(
        functools.partial(half_kernel, half, bool(given)),
        in_specs=[VMEM] * (3 + len(given)) + [VMEM] * len(first),
        out_specs=HBM,
        out_shape=pltpu.HBM((units // 2, width), BF16),
        scratch_shapes=[pltpu.VMEM((units // 2, width), BF16), pltpu.SemaphoreType.DMA((FOLD,))],
        compiler_params=PARAMS,
        cost_estimate=cost(units * (rows + few) * width, 3 * units * width),
        name="half_kept" if given else "half_sent",
    )(main_t, extra_t, payload, *given, *first)


def product_kernel(half, place_ref, main_t_ref, extra_t_ref, weights_ref, payload_ref, *refs):
    *given, main_ref, extra_ref, score_ref, acc_main, acc_extra = refs
    units, rows = main_ref.shape
    few = extra_ref.shape[1]
    source = rows // 8
    width = weights_ref.shape[1]
    part = width // FOLD
    acc_main[...] = jnp.zeros_like(acc_main)
    acc_extra[...] = jnp.zeros_like(acc_extra)

    def step(m, carry):
        cols = columns(m, part)
        weights = weights_ref[:, cols]
        acc_main[...] += dot(weights, payload_ref[:, cols], 1, 1)
        acc_extra[...] += dot(weights, unfolded(payload_ref[:, width:], m), 1, 1)
        return carry

    lax.fori_loop(0, FOLD, step, 0)
    main, extra = acc_main[...], acc_extra[...]
    main_ref[...] = main.astype(BF16)
    extra_ref[...] = extra.astype(BF16)
    span = slice(half * units, (half + 1) * units)
    main_score = jnp.sum(main * main_t_ref[span, :].astype(F32), axis=0, keepdims=True)
    extra_score = jnp.sum(extra * extra_t_ref[span, :].astype(F32), axis=0, keepdims=True)
    to_main = (iota((source, rows), 0) ^ place_ref[3]) == iota((source, rows), 1) // 8
    at_main = iota((rows, 128), 0) % 8 == iota((rows, 128), 1)
    to_extra = (iota((source, few), 0) ^ place_ref[3]) == iota((source, few), 1) % source
    at_extra = iota((few, 128), 0) // source + 8 == iota((few, 128), 1)
    score = exact_dot(jnp.where(to_main, main_score, 0.0), jnp.where(at_main, 1.0, 0.0))
    score = score + exact_dot(jnp.where(to_extra, extra_score, 0.0), jnp.where(at_extra, 1.0, 0.0))
    if given:
        score = score + given[0][...]
    score_ref[...] = score


def half_product(place, main_t, extra_t, weights, payload, half, *given):
    units, rows = main_t.shape
    few = extra_t.shape[1]
    return pl.pallas_call(
        functools.partial(product_kernel, half),
        in_specs=[SMEM] + [VMEM] * (4 + len(given)),
        out_specs=[VMEM] * 3,
        out_shape=[
            jax.ShapeDtypeStruct((units // 2, rows), BF16),
            jax.ShapeDtypeStruct((units // 2, few), BF16),
            jax.ShapeDtypeStruct((rows // 8, 128), F32),
        ],
        scratch_shapes=[pltpu.VMEM((units // 2, rows), F32), pltpu.VMEM((units // 2, few), F32)],
        compiler_params=PARAMS,
        cost_estimate=cost(units * (rows + few) * weights.shape[1], 0),
        name="product_of_other" if half else "product_of_own",
    )(place, main_t, extra_t, weights, payload, *given)


def order_kernel(shard, place_ref, own_main, own_extra, other_main, other_extra, grad_ref):
    half, rows = own_main.shape
    few = own_extra.shape[1]
    units = 2 * half
    source = rows // 8
    to_unit = permuted_units(place_ref[0], units, shard)
    column = onehot(iota((units, units), 0) == to_unit)
    here = iota((rows, rows), 0)
    turn = onehot(iota((rows, rows), 1) == (here % source) * 8 + here // source)
    keep = onehot(iota((few, few), 0) == iota((few, few), 1))
    own, other = column[:, :half], column[:, half:]
    main = (dot(own, own_main[...]) + dot(other, other_main[...])).astype(BF16)
    extra = (dot(own, own_extra[...]) + dot(other, other_extra[...])).astype(BF16)
    grad_ref[:rows, :] = dot(turn, main, 1, 1).astype(BF16)
    grad_ref[rows:, :] = dot(keep, extra, 1, 1).astype(BF16)


def exact_dot(a, b, ca=1, cb=0):
    return lax.dot_general(
        a,
        b,
        (((ca,), (cb,)), ((), ())),
        precision=lax.Precision.HIGHEST,
        preferred_element_type=F32,
    )


def placed_kernel(place_ref, *refs):
    *pieces, out_ref, sems = refs
    count = len(pieces)
    copies = []
    for k, piece in enumerate(pieces):
        base = lax.rem(place_ref[1] + k, count) * 2
        for t in range(2):
            spot = base + (place_ref[2] ^ t)
            copies.append(pltpu.make_async_copy(piece.at[t], out_ref.at[spot], sems.at[2 * k + t]))
            copies[-1].start()
    for copy in copies:
        copy.wait()


def gathered(place, pair):
    size = lax.axis_size("y")
    down = [(i, (i + size - 1) % size) for i in range(size)]
    up = [(i, (i + 1) % size) for i in range(size)]
    above = below = pair = in_hbm(pair)
    pieces = [pair] + [None] * (size - 1)
    for k in range(1, size // 2 + 1):
        above = in_hbm(lax.ppermute(above, "y", down))
        pieces[k] = above
        if k < size - k:
            below = in_hbm(lax.ppermute(below, "y", up))
            pieces[size - k] = below
    placed = pl.pallas_call(
        placed_kernel,
        in_specs=[SMEM] + [HBM] * size,
        out_specs=VMEM,
        out_shape=jax.ShapeDtypeStruct((2 * size, *pair.shape[1:]), pair.dtype),
        scratch_shapes=[pltpu.SemaphoreType.DMA((2 * size,))],
        compiler_params=PARAMS,
        cost_estimate=cost(0, 0),
        name="placed",
    )(place, *pieces)
    return placed


def pair_kernel(weights_ref, beside_ref, first_ref, out_ref):
    out_ref[0] = weights_ref[...]
    out_ref[1] = beside_ref[...]


def paired(weights, beside, first):
    return pl.pallas_call(
        pair_kernel,
        in_specs=[VMEM, VMEM, HBM],
        out_specs=VMEM,
        out_shape=jax.ShapeDtypeStruct((2, *weights.shape), weights.dtype),
        compiler_params=PARAMS,
        cost_estimate=cost(0, 0),
        name="paired",
    )(weights, beside, in_hbm(first))


def exchanged_by_bits(blocks):
    count, lanes = blocks.shape
    inner = lax.axis_size("x")
    bit = 1
    while bit < count:
        axis, step = ("x", bit) if bit < inner else ("zh", bit // inner)
        size = lax.axis_size(axis)
        pairs = blocks.reshape(count // (2 * bit), 2, bit, lanes)
        came = lax.ppermute(pairs[:, 1], axis, [(i, i ^ step) for i in range(size)])
        blocks = jnp.stack([pairs[:, 0], came], axis=1).reshape(count, lanes)
        bit *= 2
    return blocks


def in_vmem(array):
    return pltpu.with_memory_space_constraint(array, pltpu.VMEM)


def in_hbm(array):
    return pltpu.with_memory_space_constraint(array, pltpu.HBM)


def after(array, first):
    return pl.pallas_call(
        after_kernel,
        in_specs=[HBM, VMEM],
        out_specs=HBM,
        out_shape=pltpu.HBM(array.shape, array.dtype),
        input_output_aliases={0: 0},
        cost_estimate=cost(0, 0),
        name="after",
    )(array, first)


def after_kernel(array_ref, first_ref, out_ref):
    pass


def sum_kernel(pieces_ref, out_ref):
    total = pieces_ref[0].astype(F32)
    for k in range(1, pieces_ref.shape[0]):
        total = total + pieces_ref[k].astype(F32)
    out_ref[...] = total


def summed(pieces):
    count, shard, width = pieces.shape
    part = width // 4
    return pl.pallas_call(
        sum_kernel,
        grid=(4,),
        in_specs=[pl.BlockSpec((count, shard, part), lambda g: (0, 0, g))],
        out_specs=pl.BlockSpec((shard, part), lambda g: (0, g)),
        out_shape=jax.ShapeDtypeStruct((shard, width), F32),
        compiler_params=PARAMS,
        cost_estimate=cost(count * shard * width, 2 * count * shard * width),
        name="summed",
    )(pieces)


def logits_kernel(place_ref, logits_ref, chosen_ref, slots_ref, outside_ref, score_ref, out_ref):
    gating = softmax_rows(logits_ref[...])
    sent = gating.astype(BF16).astype(F32)
    chosen, slots = chosen_ref[...], slots_ref[...]
    topk, tokens = chosen.shape
    experts = score_ref.shape[0]
    returned = score_ref[:, :16]
    found = []
    here = chosen ^ place_ref[3]
    for k in range(topk):
        hit = jnp.where(iota((experts, tokens), 0) == here[k : k + 1, :], 1.0, 0.0)
        by_slot = exact_dot(returned, hit, 0, 0)
        at_slot = iota((16, tokens), 0) == slots[k : k + 1, :]
        found.append(jnp.sum(jnp.where(at_slot, by_slot, 0.0), axis=0, keepdims=True))
    inside = jnp.concatenate(found, axis=0) / sent
    outside = jnp.where(chosen >= experts, outside_ref[...], 0.0)
    scores = jnp.where(slots < 10, inside, outside)
    mean = jnp.sum(gating * scores, axis=0, keepdims=True)
    out_ref[...] = gating * (scores - mean)


def body(grad_output, logits, chosen, slots, other_scores, hidden, down_weight):
    tokens, topk = logits.shape
    window, capacity, units = hidden.shape[2], hidden.shape[3], hidden.shape[4]
    model = grad_output.shape[1]
    shard = down_weight.shape[1]
    place = jnp.stack([lax.axis_index(k) for k in ("core", "y", "zl", EXPERT)]).astype(jnp.int32)
    logits_t, chosen_t, slots_t = logits.T, chosen.T, slots.T
    swap = [(0, 1), (1, 0)]

    weights = down_weight.reshape(shard, model)
    beside = lax.ppermute(weights, "zl", swap)
    tile = jax.ShapeDtypeStruct((window * 8, tokens), BF16)
    placing = pl.pallas_call(
        place_kernel,
        in_specs=[HBM] * 3,
        out_specs=[VMEM] * 2,
        out_shape=[tile, tile],
        scratch_shapes=[
            pltpu.VMEM((topk, tokens), F32),
            pltpu.VMEM((topk, tokens), jnp.int32),
            pltpu.VMEM((topk, tokens), jnp.int32),
            pltpu.SemaphoreType.DMA((3,)),
        ],
        compiler_params=PARAMS,
        cost_estimate=cost(0, 4 * 320 * model),
        name="placing",
    )(*map(in_hbm, (logits_t, chosen_t, slots_t)))
    packed_shape = (window * 8, model + model // FOLD)
    packed = pl.pallas_call(
        pack_kernel,
        in_specs=[VMEM, VMEM, HBM],
        out_specs=HBM,
        out_shape=pltpu.HBM(packed_shape, BF16),
        scratch_shapes=[
            pltpu.VMEM((tokens, model), BF16),
            pltpu.VMEM(packed_shape, BF16),
            pltpu.SemaphoreType.DMA((FOLD + 2,)),
        ],
        compiler_params=PARAMS,
        cost_estimate=cost(2 * 320 * tokens * model * 2, 4 * 320 * model),
        name="pack",
    )(*placing, in_hbm(grad_output))
    packed = after(packed, beside[:8, :128])
    payload = lax.all_to_all(
        packed.reshape(window, 8, packed.shape[1]), EXPERT, split_axis=0, concat_axis=0, tiled=True
    ).reshape(packed.shape)

    own_weights = gathered(place, paired(weights, beside, packed))
    own_weights = own_weights.reshape(-1, model)
    other_weights = in_vmem(lax.ppermute(own_weights, "core", swap))

    by_slot = hidden.transpose(0, 1, 3, 2, 4).reshape(capacity * window, units)
    main_t, extra_t = pl.pallas_call(
        functools.partial(hidden_kernel, shard),
        in_specs=[SMEM, VMEM],
        out_specs=[VMEM] * 2,
        out_shape=[
            jax.ShapeDtypeStruct((units, window * 8), BF16),
            jax.ShapeDtypeStruct((units, window * 2), BF16),
        ],
        compiler_params=PARAMS,
        cost_estimate=cost(4 * 320 * units * units, 8 * 320 * units),
        name="hidden_order",
    )(place, by_slot)

    sent = half_partial(main_t, extra_t, payload, 1, first=(own_weights[:8, :128],))
    arrived = lax.ppermute(sent, "core", swap)
    *own_grad, score = half_product(place, main_t, extra_t, own_weights, payload, 0)
    *other_grad, score = half_product(place, main_t, extra_t, other_weights, payload, 1, score)
    both = half_partial(main_t, extra_t, payload, 0, arrived, first=(score,))
    parts = lax.all_to_all(
        both.reshape(-1, shard, model), RING, split_axis=0, concat_axis=0, tiled=True
    )
    grad_down = summed(in_vmem(parts)).reshape(1, shard, model)

    returned = exchanged_by_bits(score)
    grad = pl.pallas_call(
        functools.partial(order_kernel, shard),
        in_specs=[SMEM] + [VMEM] * 4,
        out_specs=VMEM,
        out_shape=jax.ShapeDtypeStruct((capacity * window, units), BF16),
        compiler_params=PARAMS,
        cost_estimate=cost(2 * 320 * units * units, 4 * 320 * units),
        name="order",
    )(place, *own_grad, *other_grad)
    grad_hidden = grad.reshape(1, 1, capacity, window, units).transpose(0, 1, 3, 2, 4)
    grad_logits = pl.pallas_call(
        logits_kernel,
        in_specs=[SMEM] + [VMEM] * 5,
        out_specs=VMEM,
        out_shape=jax.ShapeDtypeStruct((topk, tokens), F32),
        compiler_params=PARAMS,
        cost_estimate=cost(0, 0),
        name="logits",
    )(place, logits_t, chosen_t, slots_t, other_scores.T, returned)
    return grad_hidden, grad_down, grad_logits.T


def solution(mesh):
    torus = Mesh(mesh.devices.reshape(4, 8, 8, 2, 2), ALL)
    in_specs = (
        P(ALL, None),
        P(ALL, None),
        P(ALL, None),
        P(ALL, None),
        P(ALL, None),
        P(EXPERT, DP, None, None, None),
        P(EXPERT, DP, None),
    )
    out_specs = (P(EXPERT, DP, None, None, None), P(EXPERT, DP, None), P(ALL, None))
    return jax.shard_map(body, mesh=torus, in_specs=in_specs, out_specs=out_specs, check_vma=False)
```
